32 devices in a mesh: fsdp: 8 (over y, x, core), ctx: 4 (over z).
Axes of the slice: x: 2, y: 2, z: 4, core: 2. Of those that a mesh axis runs over, the one named last changes fastest.
Arguments:
- byte_ids: int32 [8, 4096], P('fsdp', 'ctx'), may hold values from 0 to 255
- byte_table: bfloat16 [256, 768], replicated, may hold values from -6 to 6
- w_conv: bfloat16 [3072, 1024], P('fsdp'), may hold values from -0.109375 to 0.109375
- w_qkv: bfloat16 [1024, 1536], P('fsdp'), may hold values from -4 to 4
- w_out: bfloat16 [1024, 1024], P('fsdp'), may hold values from -0.1875 to 0.1875
- norm_gain: bfloat16 [1024], replicated, may hold values from 0.5 to 1.5
- teacher: bfloat16 [8, 1024, 1024], P('fsdp', 'ctx'), may hold values from -6 to 6
- align: int32 [8, 1024], P('fsdp', 'ctx'), may hold values from 0 to 1023, as said below
Outputs:
- hidden_out: bfloat16 [8, 1024, 1024], P('fsdp', 'ctx')
- token_loss: float32 [8, 1024], P('fsdp', 'ctx')
The draws below stay inside these ranges and needn't reach their ends.
Inputs may be any that keep to these rules, and one draw needn't show every extreme that they name: Teacher token j of a sequence points at a latent of its own aligned block of 256 rows (align // 256 == j // 256); the first and the last token of each block point at that block's first and last latent.
All inputs are finite; a program needn't handle non-finite values.
Results may differ from the reference program's by a relative error of at most 0.039.
Values may be sent and summed in bfloat16 or wider, within the bound.
No kernel may reach another device: no remote copies, remote signals or barrier semaphores. Data moves between devices by JAX's collectives and lax.ppermute only.
A program may use at most 64 MiB of HBM per device.

```python
import math
import jax
import jax.numpy as jnp
import numpy as np
from jax import lax

D = 1024
E = 768
KW = 4
BYTE_VOCAB = 256
HQ = 16
HK = 4
HD = 64
LAT_DEV = 256
GROUP = 4
QKV = 1536
LATENTS = 1024
BYTES = 4096
SEQS = 8


def draw_w_qkv(key, part):
    key = jax.random.fold_in(key, 11)
    base = jax.random.truncated_normal(key, -6.0, 6.0, (D, QKV), jnp.float32) / math.sqrt(D)
    column = jnp.arange(QKV, dtype=jnp.int32)
    lift = jnp.where(column < HQ * HD + HK * HD, 2.0, 1.0).astype(jnp.float32)
    base = base * lift[None, :]
    return jnp.clip(base, -4.0, 4.0).astype(jnp.bfloat16)


def draw_align(key, part):
    key = jax.random.fold_in(key, 5)
    row_index = jnp.arange(LATENTS, dtype=jnp.int32)
    block_first = row_index // LAT_DEV * LAT_DEV
    in_block = row_index % LAT_DEV
    offsets = jax.random.randint(key, (SEQS, LATENTS), 0, LAT_DEV, dtype=jnp.int32)
    offsets = jnp.where(in_block[None, :] == 0, 0, offsets)
    offsets = jnp.where(in_block[None, :] == LAT_DEV - 1, LAT_DEV - 1, offsets)
    return (block_first[None, :] + offsets).astype(jnp.int32)


def with_ends(drawn, stream_key, least, largest):
    longest = drawn.shape.index(max(drawn.shape))
    spots = []
    for shift in (0, 1):
        where = [jax.random.randint(jax.random.fold_in(stream_key, axis), (), 0, length) for axis, length in enumerate(drawn.shape)]
        where[longest] = (where[longest] + shift) % drawn.shape[longest]
        spots.append(tuple(where))
    return drawn.at[spots[0]].set(least).at[spots[1]].set(largest)


def block_scale(own_key, dims, split, smallest, largest):
    def one(dim, parts):
        heights = jax.random.uniform(jax.random.fold_in(jax.random.fold_in(own_key, 6), dim), (parts,), jnp.float32, smallest / len(split), largest / len(split))
        return jnp.repeat(jnp.exp(heights), dims[dim] // parts).reshape((-1,) + (1,) * (len(dims) - dim - 1))

    loudness = one(*split[0])
    for cut in split[1:]:
        loudness = loudness * one(*cut)
    return loudness


def cumulative_ranks(number_of, lean):
    portions = [(1 << 20) // math.isqrt(grade ** lean) + 1 for grade in range(1, number_of + 1)]
    spread = 1 + sum(portions) // (1 << 30)
    return np.cumsum(np.array([max(1, weight // spread) for weight in portions]))


def ranked_ids(key, extent, amount, skew):
    table = cumulative_ranks(amount, skew)
    pick = jax.random.randint(jax.random.fold_in(key, 1), extent, 0, int(table[amount - 1]))
    standing = jnp.searchsorted(jnp.asarray(table, jnp.int32), pick, side="right")
    return jax.random.permutation(jax.random.fold_in(key, 2), amount)[standing].astype(jnp.int32)


def gaussian(rng, extent, scale, reach, shards=(), kind=jnp.bfloat16):
    result = jax.random.normal(rng, extent, jnp.float32) * scale
    if len(shards) > 0:
        result = block_scale(rng, extent, shards, -0.22, 0.18) * result
    return jnp.clip(result, min=-reach, max=reach).astype(kind)


def setup_inputs(seed: int = 0) -> dict:
    arg_keys = jax.random.split(jax.random.key(seed), 9)
    byte_ids = with_ends(ranked_ids(arg_keys[0], (SEQS, BYTES), BYTE_VOCAB, 2), jax.random.fold_in(arg_keys[0], 3), 0, BYTE_VOCAB - 1).astype(jnp.int32)
    byte_table = gaussian(arg_keys[1], (BYTE_VOCAB, E), 1.0, 6.0)
    w_conv = gaussian(arg_keys[2], (KW * E, D), (KW * E) ** -0.5, 0.109375, ((0, 8),))
    w_qkv = draw_w_qkv(jax.random.fold_in(arg_keys[8], 71), 0)
    w_out = gaussian(arg_keys[4], (HQ * HD, D), (HQ * HD) ** -0.5, 0.1875, ((0, 8),))
    norm_gain = jnp.clip(jax.random.uniform(arg_keys[5], (D,), jnp.float32, 0.5, 1.5), 0.5, 1.5).astype(jnp.bfloat16)
    teacher = gaussian(arg_keys[6], (SEQS, LATENTS, D), 1.0, 6.0, ((0, 8), (1, 4)))
    align = draw_align(jax.random.fold_in(arg_keys[8], 71), 0)
    return {"byte_ids": byte_ids, "byte_table": byte_table, "w_conv": w_conv, "w_qkv": w_qkv, "w_out": w_out, "norm_gain": norm_gain, "teacher": teacher, "align": align}


theta_base = 500000.0
norm_eps = 1e-05

def rotate(values, positions):
    half_dim = values.shape[-1] // 2
    frequency = theta_base ** (-jnp.arange(half_dim, dtype=jnp.float32) * 2.0 / values.shape[-1])
    angles = positions.astype(jnp.float32)[:, None] * frequency[None, :]
    angles = jnp.concatenate([angles, angles], axis=-1)[:, None, :]
    turned = jnp.concatenate([-values[..., half_dim:], values[..., :half_dim]], axis=-1)
    return values * jnp.cos(angles) + turned * jnp.sin(angles)

def reference(byte_ids, byte_table, w_conv, w_qkv, w_out, norm_gain, teacher, align):
    score_scale = 1.0 / math.sqrt(HD)
    query_width = HQ * HD
    key_width = HK * HD

    def one_sequence(inputs):
        sequence_ids, teach_rows, aligned = inputs
        embedded = byte_table[sequence_ids]
        stacked = embedded.reshape(LATENTS, KW * E)
        latent = jnp.dot(stacked, w_conv, preferred_element_type=jnp.float32).astype(jnp.bfloat16)
        latent_wide = latent.astype(jnp.float32)
        scale_rows = lax.rsqrt(lax.optimization_barrier(jnp.mean(latent_wide * latent_wide, axis=1, keepdims=True)) + norm_eps)
        normed = (latent_wide * scale_rows * norm_gain.astype(jnp.float32)[None, :]).astype(jnp.bfloat16)
        projected = jnp.dot(normed, w_qkv, preferred_element_type=jnp.float32)
        positions = jnp.arange(LATENTS, dtype=jnp.int32)
        queries = rotate(projected[:, :query_width].reshape(LATENTS, HQ, HD), positions).astype(jnp.bfloat16)
        key_rows = rotate(projected[:, query_width:query_width + key_width].reshape(LATENTS, HK, HD), positions).astype(jnp.bfloat16)
        value_rows = projected[:, query_width + key_width:].reshape(LATENTS, HK, HD).astype(jnp.bfloat16)
        allowed = positions[None, :] <= positions[:, None]

        def head_out(head):
            query_head = lax.dynamic_index_in_dim(queries, head, axis=1, keepdims=False)
            group_index = head // GROUP
            key_head = lax.dynamic_index_in_dim(key_rows, group_index, axis=1, keepdims=False)
            value_head = lax.dynamic_index_in_dim(value_rows, group_index, axis=1, keepdims=False)
            scores = jnp.dot(query_head, key_head.T, preferred_element_type=jnp.float32) * score_scale
            scores = jnp.where(allowed, scores, -jnp.inf)
            row_top = lax.optimization_barrier(jnp.max(scores, axis=1, keepdims=True))
            probs = jnp.exp(scores - row_top)
            row_mass = lax.optimization_barrier(jnp.sum(probs, axis=1, keepdims=True))
            summed = jnp.dot(probs.astype(jnp.bfloat16), value_head, preferred_element_type=jnp.float32)
            return summed / row_mass
        heads = lax.map(head_out, jnp.arange(HQ, dtype=jnp.int32))
        attended = jnp.transpose(heads, (1, 0, 2)).reshape(LATENTS, HQ * HD).astype(jnp.bfloat16)
        branch = jnp.dot(attended, w_out, preferred_element_type=jnp.float32)
        hidden_out = (latent_wide + branch).astype(jnp.bfloat16)
        picked = jnp.take(hidden_out, aligned, axis=0)
        difference = picked.astype(jnp.float32) - teach_rows.astype(jnp.float32)
        token_loss = lax.optimization_barrier(jnp.mean(difference * difference, axis=1))
        return (hidden_out, token_loss)
    hidden_all, loss_all = lax.map(one_sequence, (byte_ids, teacher, align))
    return (hidden_all, loss_all)
```

```python
import functools
import math

import jax
import jax.numpy as jnp
import numpy as np
from jax import lax
from jax.experimental import pallas as pl
from jax.experimental.pallas import tpu as pltpu
from jax.sharding import PartitionSpec as P

KW = 4
HQ = 16
HK = 4
HD = 64
GROUP = HQ // HK
VOCAB = 256

theta_base = 500000.0
norm_eps = 1e-05
masked_score = -1e30
score_scale = 1.0 / math.sqrt(HD)


def rotate(values, positions):
    half_dim = values.shape[-1] // 2
    frequency = theta_base ** (-jnp.arange(half_dim, dtype=jnp.float32) * 2.0 / values.shape[-1])
    angles = positions.astype(jnp.float32)[:, None] * frequency[None, :]
    angles = jnp.concatenate([angles, angles], axis=-1)[:, None, :]
    turned = jnp.concatenate([-values[..., half_dim:], values[..., :half_dim]], axis=-1)
    return values * jnp.cos(angles) + turned * jnp.sin(angles)


def project(inputs, weight):
    return jnp.dot(
        inputs,
        lax.all_gather(weight, "fsdp", axis=0, tiled=True),
        preferred_element_type=jnp.float32,
    )


def general_body(byte_ids, byte_table, w_conv, w_qkv, w_out, norm_gain, teacher, align):
    seq_bytes = byte_ids.shape[1]
    lat_rows = seq_bytes // KW
    query_width = HQ * HD
    key_width = HK * HD
    one_hot = (
        byte_ids[0][:, None] == jnp.arange(byte_table.shape[0], dtype=jnp.int32)[None, :]
    ).astype(jnp.bfloat16)
    embedded = jnp.dot(one_hot, byte_table, preferred_element_type=jnp.float32).astype(jnp.bfloat16)
    stacked = embedded.reshape(lat_rows, KW * byte_table.shape[1])
    latent = project(stacked, w_conv).astype(jnp.bfloat16)
    latent_wide = latent.astype(jnp.float32)
    scale_rows = lax.rsqrt(jnp.mean(latent_wide * latent_wide, axis=1, keepdims=True) + norm_eps)
    normed = (latent_wide * scale_rows * norm_gain.astype(jnp.float32)[None, :]).astype(
        jnp.bfloat16
    )
    projected = project(normed, w_qkv)
    ctx_index = lax.axis_index("ctx")
    positions = ctx_index * lat_rows + jnp.arange(lat_rows, dtype=jnp.int32)
    queries = rotate(projected[:, :query_width].reshape(lat_rows, HQ, HD), positions).astype(
        jnp.bfloat16
    )
    key_rows = rotate(
        projected[:, query_width : query_width + key_width].reshape(lat_rows, HK, HD), positions
    )
    key_rows = key_rows.astype(jnp.bfloat16).reshape(lat_rows, key_width)
    value_rows = projected[:, query_width + key_width :].astype(jnp.bfloat16)
    grouped = queries.reshape(lat_rows, HK, HQ // HK, HD)
    start_state = (
        jnp.full((HK, HQ // HK, lat_rows), masked_score, jnp.float32),
        jnp.zeros((HK, HQ // HK, lat_rows), jnp.float32),
        jnp.zeros((HK, HQ // HK, lat_rows, HD), jnp.float32),
    )
    key_all = lax.all_gather(key_rows, "ctx", axis=0, tiled=True)
    value_all = lax.all_gather(value_rows, "ctx", axis=0, tiled=True)
    blocks = key_all.shape[0] // lat_rows
    key_blocks = key_all.reshape(blocks, lat_rows, HK, HD)
    value_blocks = value_all.reshape(blocks, lat_rows, HK, HD)
    block_starts = lat_rows * jnp.arange(blocks, dtype=jnp.int32)

    def one_block(partial_value, block_data):
        key_block, value_block, key_start = block_data
        row_top, row_mass, weighted = partial_value
        scores = (
            jnp.einsum("qkgd,skd->kgqs", grouped, key_block, preferred_element_type=jnp.float32)
            * score_scale
        )
        key_pos = key_start + jnp.arange(lat_rows, dtype=jnp.int32)
        allowed = key_pos[None, :] <= positions[:, None]
        scores = jnp.where(allowed[None, None], scores, masked_score)
        new_top = jnp.maximum(row_top, jnp.max(scores, axis=-1))
        weights = jnp.exp(scores - new_top[..., None])
        shrink = jnp.exp(row_top - new_top)
        row_mass = row_mass * shrink + jnp.sum(weights, axis=-1)
        weighted = weighted * shrink[..., None] + jnp.einsum(
            "kgqs,skd->kgqd",
            weights.astype(jnp.bfloat16),
            value_block,
            preferred_element_type=jnp.float32,
        )
        return ((new_top, row_mass, weighted), None)

    result, unused = lax.scan(one_block, start_state, (key_blocks, value_blocks, block_starts))
    final_top, final_mass, final_sum = result
    attended = final_sum / final_mass[..., None]
    attended = jnp.transpose(attended, (2, 0, 1, 3)).reshape(lat_rows, HQ * HD).astype(jnp.bfloat16)
    branch = project(attended, w_out)
    hidden_out = (latent_wide + branch).astype(jnp.bfloat16)
    local_rows = align[0] - ctx_index * lat_rows
    picked = jnp.take(hidden_out, local_rows, axis=0)
    difference = picked.astype(jnp.float32) - teacher[0].astype(jnp.float32)
    token_loss = jnp.mean(difference * difference, axis=1)
    return (hidden_out[None], token_loss[None])


def rope_tables(length):
    half = HD // 2
    frequency = np.float32(theta_base) ** (-np.arange(half, dtype=np.float32) * np.float32(2.0 / HD))
    angles = np.arange(length, dtype=np.float32)[:, None] * frequency[None, :]
    angles = angles.astype(np.float64)
    cos, sin = np.cos(angles).astype(np.float32), np.sin(angles).astype(np.float32)
    return np.concatenate([cos] * 4, axis=1), np.concatenate([-sin, sin] * 2, axis=1)


def turn(x, cos, sin):
    half = HD // 2
    lane = lax.broadcasted_iota(jnp.int32, x.shape, 1)
    low = (lane & half) == 0
    swapped = jnp.where(low, pltpu.roll(x, 128 - half, axis=1), pltpu.roll(x, half, axis=1))
    return x * cos + swapped * sin


def own_kernel(where_ref, bytes_ref, conv_ref, qkv_ref, total_ref, part_ref):
    core, ctx = where_ref[1], where_ref[2]
    taps_in = conv_ref.shape[0]
    half = total_ref.shape[0]
    rows = pl.ds(pl.multiple_of(core * half, half), half)
    mine = bytes_ref[rows, pl.ds(pl.multiple_of(core * taps_in, taps_in), taps_in)]
    total_ref[...] = jnp.dot(mine, conv_ref[...], preferred_element_type=jnp.float32)
    q_width = GROUP * HD
    part_ref[:, :q_width] = qkv_ref[:, pl.ds(pl.multiple_of(ctx * q_width, q_width), q_width)]
    heads = []
    for start in (HQ * HD, HQ * HD + HK * HD):
        pair = qkv_ref[:, pl.ds(pl.multiple_of(start + ctx // 2 * 128, 128), 128)].astype(jnp.float32)
        heads.append(jnp.where(ctx % 2 == 1, pltpu.roll(pair, HD, axis=1), pair)[:, :HD])
    part_ref[:, q_width:] = jnp.concatenate(heads, axis=1).astype(jnp.bfloat16)


def mate_kernel(where_ref, bytes_ref, conv_ref, total_ref, part_ref, out_ref):
    core = where_ref[1]
    taps_in = conv_ref.shape[0]
    half, width = total_ref.shape
    rows = pl.ds(pl.multiple_of(core * half, half), half)
    mates = bytes_ref[rows, pl.ds(pl.multiple_of((1 - core) * taps_in, taps_in), taps_in)]
    total = total_ref[...] + jnp.dot(mates, conv_ref[...], preferred_element_type=jnp.float32)
    out_ref[:, :width] = total.astype(jnp.bfloat16)
    out_ref[:, width:] = part_ref[...]


def ordered(chip, core, pieces):
    own, near, mate_own, mate_near = pieces
    depth = own.shape[0]
    for j, (mine, mates) in enumerate(zip((own,) + near, (mate_own,) + mate_near)):
        base = (chip ^ j) * 2
        for which, piece in ((core, mine), (1 - core, mates)):
            yield pl.ds(pl.multiple_of((base + which) * depth, depth), depth), piece


def attend_kernel(
    where_ref, ids_refs, own, near, mate_own, mate_near, gain_ref, cos_ref, sin_ref, att_ref, lat_ref,
    table_s, weight_s, ids_s, lat_s, q_s, k_s, v_s,
):
    chip, core, ctx = where_ref[0], where_ref[1], where_ref[2]
    blocks, rows = len(ids_refs), ids_refs[0].shape[1]
    features = lat_ref.shape[1]
    for span, piece in ordered(chip, core, (own, near, mate_own, mate_near)):
        table_s[span, :] = piece[:, :features]
        weight_s[span, :] = piece[:, features:]
    for d, ids in enumerate(ids_refs):
        ids_s[(ctx - d) & (blocks - 1)] = ids[...]
    gain = gain_ref[...].astype(jnp.float32)
    q_width = GROUP * HD
    v_s[:, HD:, :] = jnp.ones((blocks, v_s.shape[1] - HD, rows), jnp.bfloat16)

    def lift(i):
        span = slice(i * rows, (i + 1) * rows)
        ids = jnp.transpose(ids_s[i])
        byte = lax.broadcasted_iota(jnp.int32, (rows, VOCAB), 1)
        one_hot = jnp.concatenate(
            [(ids[:, k : k + 1] == byte).astype(jnp.float32).astype(jnp.bfloat16) for k in range(KW)], axis=1
        )
        latent = jnp.dot(one_hot, table_s[...], preferred_element_type=jnp.float32).astype(jnp.bfloat16)
        lat_s[i] = latent
        wide = latent.astype(jnp.float32)
        scale = lax.rsqrt(jnp.mean(wide * wide, axis=1, keepdims=True) + norm_eps)
        normed = (wide * scale * gain).astype(jnp.bfloat16)
        projected = jnp.dot(normed, weight_s[...], preferred_element_type=jnp.float32)
        cos, sin = cos_ref[span, :], sin_ref[span, :]
        for pair in range(GROUP // 2):
            turned = turn(projected[:, pair * 128 : (pair + 1) * 128], cos, sin)
            turned = (turned * score_scale).astype(jnp.bfloat16)
            q_s[i, 2 * pair] = turned[:, :HD]
            q_s[i, 2 * pair + 1] = turned[:, HD:]
        last = projected[:, q_width:]
        k_s[span, :] = turn(last, cos, sin)[:, :HD].astype(jnp.bfloat16)
        v_s[i, :HD, :] = jnp.transpose(last)[HD:].astype(jnp.bfloat16)

    allowed = lax.broadcasted_iota(jnp.int32, (rows, rows), 0) <= lax.broadcasted_iota(
        jnp.int32, (rows, rows), 1
    )

    def one_head(i, h):
        query = q_s[i, h]
        scores = [
            lax.dot_general(
                k_s[j * rows : (j + 1) * rows, :], query, (((1,), (1,)), ((), ())),
                preferred_element_type=jnp.float32,
            )
            for j in range(i + 1)
        ]
        scores[i] = jnp.where(allowed, scores[i], masked_score)
        top = functools.reduce(jnp.maximum, [jnp.max(s, axis=0, keepdims=True) for s in scores])
        total = None
        for j, s in enumerate(scores):
            probs = jnp.exp(s - top).astype(jnp.bfloat16)
            term = jnp.dot(v_s[j], probs, preferred_element_type=jnp.float32)
            total = term if total is None else total + term
        return total[:HD] / total[HD : HD + 1]

    for i in range(blocks):
        lift(i)
    lat_ref[...] = lat_s[ctx]
    for i in range(blocks):
        slot = (i - ctx) & (blocks - 1)
        for pair in range(GROUP // 2):
            result = jnp.concatenate([one_head(i, 2 * pair), one_head(i, 2 * pair + 1)], axis=0)
            att_ref[slot, :, pair * 2 * HD : (pair + 1) * 2 * HD] = jnp.transpose(result).astype(jnp.bfloat16)


def out_kernel(
    where_ref, att_refs, own, near, mate_own, mate_near, lat_ref, teacher_ref, align_ref,
    hidden_ref, loss_ref, att_s, weight_s,
):
    chip, core, ctx = where_ref[0], where_ref[1], where_ref[2]
    rows, width = lat_ref.shape
    part = att_refs[0].shape[1]
    for span, piece in ordered(chip, core, (own, near, mate_own, mate_near)):
        weight_s[span, :] = piece[...]
    for j, att in enumerate(att_refs):
        group = (ctx - j) & (len(att_refs) - 1)
        att_s[:, pl.ds(pl.multiple_of(group * part, part), part)] = att[...]
    branch = jnp.dot(att_s[...], weight_s[...], preferred_element_type=jnp.float32)
    hidden = (lat_ref[...].astype(jnp.float32) + branch).astype(jnp.bfloat16)
    hidden_ref[...] = hidden
    source = lax.broadcasted_iota(jnp.int32, (rows, rows), 0) + ctx * rows
    chosen = (source == align_ref[...]).astype(jnp.float32).astype(jnp.bfloat16)
    picked = lax.dot_general(
        chosen, hidden, (((0,), (0,)), ((), ())), preferred_element_type=jnp.float32
    )
    difference = picked - teacher_ref[...].astype(jnp.float32)
    square = difference * difference
    lanes = square[:, :128]
    for start in range(128, width, 128):
        lanes = lanes + square[:, start : start + 128]
    loss_ref[...] = jnp.sum(jnp.transpose(lanes), axis=0, keepdims=True) * (1.0 / width)


VMEM = pl.BlockSpec(memory_space=pltpu.VMEM)
SMEM = pl.BlockSpec(memory_space=pltpu.SMEM)
MIB = 1024 * 1024


def call(kernel, name, mib, flops, in_specs, outs, scratch=()):
    return pl.pallas_call(
        kernel,
        out_shape=tuple(jax.ShapeDtypeStruct(shape, dtype) for shape, dtype in outs),
        in_specs=in_specs,
        out_specs=(VMEM,) * len(outs),
        scratch_shapes=[pltpu.VMEM(shape, dtype) for shape, dtype in scratch],
        compiler_params=pltpu.CompilerParams(vmem_limit_bytes=mib * MIB),
        cost_estimate=pl.CostEstimate(flops=flops, bytes_accessed=4 * MIB, transcendentals=0),
        name=name,
    )


def head_body(sizes, byte_ids, byte_table, w_conv, w_qkv, w_out, norm_gain, teacher, align):
    n_fsdp, n_ctx = sizes
    me, ctx = lax.axis_index("fsdp"), lax.axis_index("ctx")
    chip, core = me // 2, me % 2
    rows = byte_ids.shape[1] // KW
    length = rows * n_ctx
    features = w_conv.shape[1]
    q_width = GROUP * HD
    part_width = q_width + 2 * HD
    half = VOCAB // 2
    bf16, f32 = jnp.bfloat16, jnp.float32
    where = jnp.stack([chip, core, ctx]).astype(jnp.int32)

    def swap(x, j):
        return lax.ppermute(x, "fsdp", [(d, d ^ j) for d in range(n_fsdp)])

    def along(x, d):
        return lax.ppermute(x, "ctx", [(s, (s + d) % n_ctx) for s in range(n_ctx)])

    def to_near(x):
        return tuple(swap(x, 2 * j) for j in range(1, n_fsdp // 2))

    mate_conv = swap(w_conv, 1)
    total, part = call(
        own_kernel, "own_rows", 8, 10**9, [SMEM, VMEM, VMEM, VMEM],
        [((half, features), f32), ((w_qkv.shape[0], part_width), bf16)],
    )(where, byte_table, w_conv, w_qkv)
    (own,) = call(
        mate_kernel, "tap_table", 8, 10**8, [SMEM, VMEM, VMEM, VMEM, VMEM],
        [((half, features + part_width), bf16)],
    )(where, byte_table, mate_conv, total, part)
    near = to_near(own)

    ids = jnp.transpose(byte_ids[0].reshape(rows, KW))
    ids = jnp.pad(ids, ((0, 8 - KW), (0, 0)))
    ids, unused = lax.optimization_barrier((ids, own))
    ids_all = (ids,) + tuple(along(ids, d) for d in range(1, n_ctx))
    last, ids_all = lax.optimization_barrier((near[-1], ids_all))
    near = near[:-1] + (last,)
    pieces = (own, near, swap(own, 1), tuple(swap(piece, 1) for piece in near))
    out_own, unused = lax.optimization_barrier((w_out, near))
    out_near = to_near(out_own)

    cos, sin = rope_tables(length)
    near_specs = (VMEM,) * (n_fsdp // 2 - 1)
    piece_specs = [VMEM, near_specs, VMEM, near_specs]
    att, latent = call(
        attend_kernel, "attend", 24, 6 * 10**9,
        [SMEM, (VMEM,) * n_ctx] + piece_specs + [VMEM, VMEM, VMEM],
        [((n_ctx, rows, q_width), bf16), ((rows, features), bf16)],
        [
            ((KW * VOCAB, features), bf16),
            ((features, part_width), bf16),
            ((n_ctx, 8, rows), jnp.int32),
            ((n_ctx, rows, features), bf16),
            ((n_ctx, GROUP, rows, HD), bf16),
            ((length, HD), bf16),
            ((n_ctx, HD + 16, rows), bf16),
        ],
    )(where, ids_all, *pieces, norm_gain[None], jnp.asarray(cos), jnp.asarray(sin))

    att, out_near = lax.optimization_barrier((att, out_near))
    parts = (att[0],) + tuple(along(att[d], d) for d in range(1, n_ctx))
    first, out_near = lax.optimization_barrier((parts[1], out_near))
    parts = (parts[0], first) + parts[2:]
    out_pieces = (out_own, out_near, swap(out_own, 1), tuple(swap(piece, 1) for piece in out_near))
    hidden, loss = call(
        out_kernel, "project_out", 16, 10**9,
        [SMEM, (VMEM,) * n_ctx] + piece_specs + [VMEM, VMEM, VMEM],
        [((rows, features), bf16), ((1, rows), f32)],
        [((rows, features), bf16), ((features, features), bf16)],
    )(where, parts, *out_pieces, latent, teacher[0], align)
    return hidden[None], loss


def solution(mesh):
    in_specs = (
        P("fsdp", "ctx"),
        P(),
        P("fsdp", None),
        P("fsdp", None),
        P("fsdp", None),
        P(),
        P("fsdp", "ctx", None),
        P("fsdp", "ctx"),
    )
    out_specs = (P("fsdp", "ctx", None), P("fsdp", "ctx"))
    sizes = (mesh.shape["fsdp"], mesh.shape["ctx"])
    body = functools.partial(head_body, sizes) if sizes == (2 * KW, HK) else general_body
    return jax.shard_map(body, mesh=mesh, in_specs=in_specs, out_specs=out_specs, check_vma=False)
```

```python
import functools
import math

import jax
import jax.numpy as jnp
import numpy as np
from jax import lax
from jax.experimental import pallas as pl
from jax.experimental.pallas import tpu as pltpu
from jax.sharding import PartitionSpec as P

KW = 4
HQ = 16
HK = 4
HD = 64
GROUP = HQ // HK
VOCAB = 256

theta_base = 500000.0
norm_eps = 1e-05
masked_score = -1e30
score_scale = 1.0 / math.sqrt(HD)


def rotate(values, positions):
    half_dim = values.shape[-1] // 2
    frequency = theta_base ** (-jnp.arange(half_dim, dtype=jnp.float32) * 2.0 / values.shape[-1])
    angles = positions.astype(jnp.float32)[:, None] * frequency[None, :]
    angles = jnp.concatenate([angles, angles], axis=-1)[:, None, :]
    turned = jnp.concatenate([-values[..., half_dim:], values[..., :half_dim]], axis=-1)
    return values * jnp.cos(angles) + turned * jnp.sin(angles)


def project(inputs, weight):
    return jnp.dot(
        inputs,
        lax.all_gather(weight, "fsdp", axis=0, tiled=True),
        preferred_element_type=jnp.float32,
    )


def general_body(byte_ids, byte_table, w_conv, w_qkv, w_out, norm_gain, teacher, align):
    seq_bytes = byte_ids.shape[1]
    lat_rows = seq_bytes // KW
    query_width = HQ * HD
    key_width = HK * HD
    one_hot = (
        byte_ids[0][:, None] == jnp.arange(byte_table.shape[0], dtype=jnp.int32)[None, :]
    ).astype(jnp.bfloat16)
    embedded = jnp.dot(one_hot, byte_table, preferred_element_type=jnp.float32).astype(jnp.bfloat16)
    stacked = embedded.reshape(lat_rows, KW * byte_table.shape[1])
    latent = project(stacked, w_conv).astype(jnp.bfloat16)
    latent_wide = latent.astype(jnp.float32)
    scale_rows = lax.rsqrt(jnp.mean(latent_wide * latent_wide, axis=1, keepdims=True) + norm_eps)
    normed = (latent_wide * scale_rows * norm_gain.astype(jnp.float32)[None, :]).astype(
        jnp.bfloat16
    )
    projected = project(normed, w_qkv)
    ctx_index = lax.axis_index("ctx")
    positions = ctx_index * lat_rows + jnp.arange(lat_rows, dtype=jnp.int32)
    queries = rotate(projected[:, :query_width].reshape(lat_rows, HQ, HD), positions).astype(
        jnp.bfloat16
    )
    key_rows = rotate(
        projected[:, query_width : query_width + key_width].reshape(lat_rows, HK, HD), positions
    )
    key_rows = key_rows.astype(jnp.bfloat16).reshape(lat_rows, key_width)
    value_rows = projected[:, query_width + key_width :].astype(jnp.bfloat16)
    grouped = queries.reshape(lat_rows, HK, HQ // HK, HD)
    start_state = (
        jnp.full((HK, HQ // HK, lat_rows), masked_score, jnp.float32),
        jnp.zeros((HK, HQ // HK, lat_rows), jnp.float32),
        jnp.zeros((HK, HQ // HK, lat_rows, HD), jnp.float32),
    )
    key_all = lax.all_gather(key_rows, "ctx", axis=0, tiled=True)
    value_all = lax.all_gather(value_rows, "ctx", axis=0, tiled=True)
    blocks = key_all.shape[0] // lat_rows
    key_blocks = key_all.reshape(blocks, lat_rows, HK, HD)
    value_blocks = value_all.reshape(blocks, lat_rows, HK, HD)
    block_starts = lat_rows * jnp.arange(blocks, dtype=jnp.int32)

    def one_block(partial_value, block_data):
        key_block, value_block, key_start = block_data
        row_top, row_mass, weighted = partial_value
        scores = (
            jnp.einsum("qkgd,skd->kgqs", grouped, key_block, preferred_element_type=jnp.float32)
            * score_scale
        )
        key_pos = key_start + jnp.arange(lat_rows, dtype=jnp.int32)
        allowed = key_pos[None, :] <= positions[:, None]
        scores = jnp.where(allowed[None, None], scores, masked_score)
        new_top = jnp.maximum(row_top, jnp.max(scores, axis=-1))
        weights = jnp.exp(scores - new_top[..., None])
        shrink = jnp.exp(row_top - new_top)
        row_mass = row_mass * shrink + jnp.sum(weights, axis=-1)
        weighted = weighted * shrink[..., None] + jnp.einsum(
            "kgqs,skd->kgqd",
            weights.astype(jnp.bfloat16),
            value_block,
            preferred_element_type=jnp.float32,
        )
        return ((new_top, row_mass, weighted), None)

    result, unused = lax.scan(one_block, start_state, (key_blocks, value_blocks, block_starts))
    final_top, final_mass, final_sum = result
    attended = final_sum / final_mass[..., None]
    attended = jnp.transpose(attended, (2, 0, 1, 3)).reshape(lat_rows, HQ * HD).astype(jnp.bfloat16)
    branch = project(attended, w_out)
    hidden_out = (latent_wide + branch).astype(jnp.bfloat16)
    local_rows = align[0] - ctx_index * lat_rows
    picked = jnp.take(hidden_out, local_rows, axis=0)
    difference = picked.astype(jnp.float32) - teacher[0].astype(jnp.float32)
    token_loss = jnp.mean(difference * difference, axis=1)
    return (hidden_out[None], token_loss[None])


def rope_tables(length):
    half = HD // 2
    frequency = np.float32(theta_base) ** (-np.arange(half, dtype=np.float32) * np.float32(2.0 / HD))
    angles = np.arange(length, dtype=np.float32)[:, None] * frequency[None, :]
    angles = angles.astype(np.float64)
    cos, sin = np.cos(angles).astype(np.float32), np.sin(angles).astype(np.float32)
    return np.concatenate([cos] * 4, axis=1), np.concatenate([-sin, sin] * 2, axis=1)


def turn(x, cos, sin):
    half = HD // 2
    lane = lax.broadcasted_iota(jnp.int32, x.shape, 1)
    low = (lane & half) == 0
    swapped = jnp.where(low, pltpu.roll(x, 128 - half, axis=1), pltpu.roll(x, half, axis=1))
    return x * cos + swapped * sin


def part_kernel(where_ref, qkv_ref, align_ref, part_ref, align_out):
    align_out[...] = align_ref[...]
    side = where_ref[2] % 2
    start = 0
    for width in (HQ * HD, HK * HD, HK * HD):
        own = width // 2
        part_ref[:, start // 2 : start // 2 + own] = qkv_ref[
            :, pl.ds(pl.multiple_of(start + side * own, own), own)
        ]
        start += width


def table_kernel(where_ref, bytes_ref, conv_ref, total_ref, out_ref):
    core = where_ref[1]
    taps_in = conv_ref.shape[0]
    half = total_ref.shape[0]
    rows = pl.ds(pl.multiple_of(core * half, half), half)
    mates = bytes_ref[rows, pl.ds(pl.multiple_of((1 - core) * taps_in, taps_in), taps_in)]
    total = total_ref[...] + jnp.dot(mates, conv_ref[...], preferred_element_type=jnp.float32)
    out_ref[...] = total.astype(jnp.bfloat16)


def ordered(chip, core, pieces):
    own, near, mate_own, mate_near = pieces
    depth = own.shape[0]
    for j, (mine, mates) in enumerate(zip((own,) + near, (mate_own,) + mate_near)):
        base = (chip ^ j) * 2
        for which, piece in ((core, mine), (1 - core, mates)):
            yield pl.ds(pl.multiple_of((base + which) * depth, depth), depth), piece


def attend(queries, key_slots, allowed, k_s, v_s, att_ref):
    heads = HQ // 2

    def one_head(h):
        query = queries(h)
        group = h // GROUP
        scores = [
            lax.dot_general(
                k_s[slot, group], query, (((1,), (1,)), ((), ())), preferred_element_type=jnp.float32
            )
            for slot in key_slots
        ]
        scores[-1] = jnp.where(allowed, scores[-1], masked_score)
        top = functools.reduce(jnp.maximum, [jnp.max(s, axis=0, keepdims=True) for s in scores])
        total = None
        for slot, s in zip(key_slots, scores):
            probs = jnp.exp(s - top).astype(jnp.bfloat16)
            term = jnp.dot(v_s[slot, group], probs, preferred_element_type=jnp.float32)
            total = term if total is None else total + term
        return total[:HD] / total[HD : HD + 1]

    for pair in range(heads // 2):
        result = jnp.concatenate([one_head(2 * pair), one_head(2 * pair + 1)], axis=0)
        att_ref[:, pair * 2 * HD : (pair + 1) * 2 * HD] = jnp.transpose(result).astype(jnp.bfloat16)


def causal(rows):
    return lax.broadcasted_iota(jnp.int32, (rows, rows), 0) <= lax.broadcasted_iota(
        jnp.int32, (rows, rows), 1
    )


def key_variants(ctx, which):
    for block in range(2):
        now = tuple(range(2, 3 + block))
        yield (which == block) & (ctx < 2), block, now
        yield (which == block) & (ctx >= 2), block, (0, 1) + now


def lift_kernel(
    where_ref, ids_ref, own_t, near_t, mate_own_t, mate_near_t, own_w, near_w, mate_own_w, mate_near_w,
    gain_ref, cos_ref, sin_ref, att_ref, query_ref, k_s, v_s, lat_ref,
    table_s, weight_s, ids_s, lat_s, q_s,
):
    chip, core, ctx = where_ref[0], where_ref[1], where_ref[2]
    side, upper = ctx % 2, ctx // 2
    rows, features = lat_ref.shape
    q_width, k_width = HQ * HD // 2, HK * HD // 2
    for span, piece in ordered(chip, core, (own_t, near_t, mate_own_t, mate_near_t)):
        table_s[span, :] = piece[...]
    for span, piece in ordered(chip, core, (own_w, near_w, mate_own_w, mate_near_w)):
        weight_s[span, :] = piece[...]
    for place, slot in enumerate((2 + side, 3 - side, side, 1 - side)):
        ids_s[slot] = ids_ref[place]
    gain = gain_ref[...].astype(jnp.float32)
    v_s[:, :, HD:, :] = jnp.ones(v_s.shape[:2] + (v_s.shape[2] - HD, rows), jnp.bfloat16)

    def lift(slot):
        ids = jnp.transpose(ids_s[slot])
        byte = lax.broadcasted_iota(jnp.int32, (rows, VOCAB), 1)
        one_hot = jnp.concatenate(
            [(ids[:, k : k + 1] == byte).astype(jnp.float32).astype(jnp.bfloat16) for k in range(KW)], axis=1
        )
        latent = jnp.dot(one_hot, table_s[...], preferred_element_type=jnp.float32).astype(jnp.bfloat16)
        wide = latent.astype(jnp.float32)
        scale = lax.rsqrt(jnp.mean(wide * wide, axis=1, keepdims=True) + norm_eps)
        normed = (wide * scale * gain).astype(jnp.bfloat16)
        block = slot if slot < 2 else 2 * upper + slot - 2
        cos, sin = cos_ref[block], sin_ref[block]
        if slot >= 2:
            lat_s[slot - 2] = latent
            asked = jnp.dot(normed, weight_s[:, :q_width], preferred_element_type=jnp.float32)
            for pair in range(q_width // 128):
                turned = turn(asked[:, pair * 128 : (pair + 1) * 128], cos, sin)
                turned = (turned * score_scale).astype(jnp.bfloat16)
                q_s[slot - 2, 2 * pair] = turned[:, :HD]
                q_s[slot - 2, 2 * pair + 1] = turned[:, HD:]
        kept = jnp.dot(normed, weight_s[:, q_width:], preferred_element_type=jnp.float32)
        keys = turn(kept[:, :k_width], cos, sin).astype(jnp.bfloat16)
        values = jnp.transpose(kept[:, k_width:]).astype(jnp.bfloat16)
        for group in range(2):
            k_s[slot, group] = keys[:, group * HD : (group + 1) * HD]
            v_s[slot, group, :HD, :] = values[group * HD : (group + 1) * HD]

    @pl.when(upper == 1)
    def _():
        lift(0)
        lift(1)

    lift(2)
    lift(3)
    lat_ref[...] = lat_s[side]
    query_ref[...] = q_s[side]
    allowed = causal(rows)
    other = 1 - side
    for condition, block, slots in key_variants(ctx, other):

        @pl.when(condition)
        def _(block=block, slots=slots):
            attend(lambda h: q_s[block, h], slots, allowed, k_s, v_s, att_ref)


def own_kernel(where_ref, query_ref, k_ref, v_ref, att_ref):
    ctx = where_ref[2]
    allowed = causal(att_ref.shape[0])
    for condition, block, slots in key_variants(ctx, ctx % 2):

        @pl.when(condition)
        def _(slots=slots):
            attend(lambda h: query_ref[h], slots, allowed, k_ref, v_ref, att_ref)


def out_kernel(
    where_ref, own_att, mate_att, own, near, mate_own, mate_near, lat_ref, teacher_ref, align_ref,
    hidden_ref, loss_ref, att_s, weight_s,
):
    chip, core, ctx = where_ref[0], where_ref[1], where_ref[2]
    side = ctx % 2
    rows, width = lat_ref.shape
    part = own_att.shape[1]
    for span, piece in ordered(chip, core, (own, near, mate_own, mate_near)):
        weight_s[span, :] = piece[...]
    att_s[:, pl.ds(pl.multiple_of(side * part, part), part)] = own_att[...]
    att_s[:, pl.ds(pl.multiple_of((1 - side) * part, part), part)] = mate_att[...]
    branch = jnp.dot(att_s[...], weight_s[...], preferred_element_type=jnp.float32)
    hidden = (lat_ref[...].astype(jnp.float32) + branch).astype(jnp.bfloat16)
    hidden_ref[...] = hidden
    source = lax.broadcasted_iota(jnp.int32, (rows, rows), 0) + ctx * rows
    chosen = (source == align_ref[...]).astype(jnp.float32).astype(jnp.bfloat16)
    picked = lax.dot_general(
        chosen, hidden, (((0,), (0,)), ((), ())), preferred_element_type=jnp.float32
    )
    difference = picked - teacher_ref[...].astype(jnp.float32)
    square = difference * difference
    lanes = square[:, :128]
    for start in range(128, width, 128):
        lanes = lanes + square[:, start : start + 128]
    loss_ref[...] = jnp.sum(jnp.transpose(lanes), axis=0, keepdims=True) * (1.0 / width)


VMEM = pl.BlockSpec(memory_space=pltpu.VMEM)
SMEM = pl.BlockSpec(memory_space=pltpu.SMEM)
MIB = 1024 * 1024


def call(kernel, name, mib, flops, in_specs, outs, scratch=()):
    return pl.pallas_call(
        kernel,
        out_shape=tuple(jax.ShapeDtypeStruct(shape, dtype) for shape, dtype in outs),
        in_specs=in_specs,
        out_specs=(VMEM,) * len(outs),
        scratch_shapes=[pltpu.VMEM(shape, dtype) for shape, dtype in scratch],
        compiler_params=pltpu.CompilerParams(vmem_limit_bytes=mib * MIB),
        cost_estimate=pl.CostEstimate(flops=flops, bytes_accessed=4 * MIB, transcendentals=0),
        name=name,
    )


def head_body(sizes, byte_ids, byte_table, w_conv, w_qkv, w_out, norm_gain, teacher, align):
    n_fsdp, n_ctx = sizes
    me, ctx = lax.axis_index("fsdp"), lax.axis_index("ctx")
    chip, core = me // 2, me % 2
    rows = byte_ids.shape[1] // KW
    features = w_conv.shape[1]
    q_width = HQ * HD // 2
    part_width = w_qkv.shape[1] // 2
    half = VOCAB // 2
    bf16, f32 = jnp.bfloat16, jnp.float32
    where = jnp.stack([chip, core, ctx]).astype(jnp.int32)

    def swap(x, j):
        return lax.ppermute(x, "fsdp", [(d, d ^ j) for d in range(n_fsdp)])

    def along(x, pairs):
        return lax.ppermute(x, "ctx", pairs)

    def to_near(x):
        return tuple(swap(x, 2 * j) for j in range(1, n_fsdp // 2))

    def to_mate(x, near):
        return x, near, swap(x, 1), tuple(swap(piece, 1) for piece in near)

    beside = [(z, z ^ 1) for z in range(n_ctx)]

    mate_conv = swap(w_conv, 1)
    part, align = call(
        part_kernel, "qkv_part", 4, 10**8, [SMEM, VMEM, VMEM],
        [((w_qkv.shape[0], part_width), bf16), (align.shape, jnp.int32)],
    )(where, w_qkv, align)
    near_w = to_near(part)

    taps_in = w_conv.shape[0]
    mine = lax.dynamic_slice(byte_table, (core * half, core * taps_in), (half, taps_in))
    total = jnp.dot(mine, w_conv, preferred_element_type=f32)
    (own_t,) = call(
        table_kernel, "tap_table", 8, 10**8, [SMEM, VMEM, VMEM, VMEM], [((half, features), bf16)]
    )(where, byte_table, mate_conv, total)
    ids_all = (
        byte_ids,
        along(byte_ids, beside),
        along(byte_ids, [(0, 2), (1, 3)]),
        along(byte_ids, [(0, 3), (1, 2)]),
    )
    own_t, ids_all = lax.optimization_barrier((own_t, ids_all))
    near_t = to_near(own_t)
    ids_all = jnp.concatenate(ids_all, axis=0).reshape(4, rows, KW)
    ids_all = jnp.pad(jnp.swapaxes(ids_all, 1, 2), ((0, 0), (0, 8 - KW), (0, 0)))
    w_pieces, mate_own_t = to_mate(part, near_w), swap(own_t, 1)
    near_t, w_pieces, mate_own_t = lax.optimization_barrier((near_t, w_pieces, mate_own_t))
    t_pieces = (own_t, near_t, mate_own_t, tuple(swap(piece, 1) for piece in near_t))
    out_own, unused = lax.optimization_barrier((w_out, near_t))
    out_near = to_near(out_own)

    cos, sin = (jnp.asarray(t.reshape(n_ctx, rows, 128)) for t in rope_tables(rows * n_ctx))
    near_specs = (VMEM,) * (n_fsdp // 2 - 1)
    piece_specs = [VMEM, near_specs, VMEM, near_specs]
    att_shape = ((rows, q_width), bf16)
    att_mate, query, keys, values, latent = call(
        lift_kernel, "lift", 28, 5 * 10**9,
        [SMEM, VMEM] + piece_specs + piece_specs + [VMEM, VMEM, VMEM],
        [
            att_shape,
            ((HQ // 2, rows, HD), bf16),
            ((4, 2, rows, HD), bf16),
            ((4, 2, HD + 16, rows), bf16),
            ((rows, features), bf16),
        ],
        [
            ((KW * VOCAB, features), bf16),
            ((features, part_width), bf16),
            ((4, 8, rows), jnp.int32),
            ((2, rows, features), bf16),
            ((2, HQ // 2, rows, HD), bf16),
        ],
    )(where, ids_all, *t_pieces, *w_pieces, norm_gain[None], cos, sin)

    att_mate, out_near = lax.optimization_barrier((att_mate, out_near))
    att_back = along(att_mate, beside)
    (att_own,) = call(
        own_kernel, "own_block", 16, 3 * 10**9, [SMEM, VMEM, VMEM, VMEM], [att_shape]
    )(where, query, keys, values)
    hidden, loss = call(
        out_kernel, "project_out", 16, 10**9,
        [SMEM, VMEM, VMEM] + piece_specs + [VMEM, VMEM, VMEM],
        [((rows, features), bf16), ((1, rows), f32)],
        [((rows, features), bf16), ((features, features), bf16)],
    )(where, att_own, att_back, *to_mate(out_own, out_near), latent, teacher[0], align)
    return hidden[None], loss


def solution(mesh):
    in_specs = (
        P("fsdp", "ctx"),
        P(),
        P("fsdp", None),
        P("fsdp", None),
        P("fsdp", None),
        P(),
        P("fsdp", "ctx", None),
        P("fsdp", "ctx"),
    )
    out_specs = (P("fsdp", "ctx", None), P("fsdp", "ctx"))
    sizes = (mesh.shape["fsdp"], mesh.shape["ctx"])
    body = functools.partial(head_body, sizes) if sizes == (2 * KW, HK) else general_body
    return jax.shard_map(body, mesh=mesh, in_specs=in_specs, out_specs=out_specs, check_vma=False)
```

```python
import functools
import math

import jax
import jax.numpy as jnp
import numpy as np
from jax import lax
from jax.experimental import pallas as pl
from jax.experimental.pallas import tpu as pltpu
from jax.sharding import PartitionSpec as P

KW = 4
HQ = 16
HK = 4
HD = 64
GROUP = HQ // HK
VOCAB = 256

theta_base = 500000.0
norm_eps = 1e-05
masked_score = -1e30
score_scale = 1.0 / math.sqrt(HD)


def rotate(values, positions):
    half_dim = values.shape[-1] // 2
    frequency = theta_base ** (-jnp.arange(half_dim, dtype=jnp.float32) * 2.0 / values.shape[-1])
    angles = positions.astype(jnp.float32)[:, None] * frequency[None, :]
    angles = jnp.concatenate([angles, angles], axis=-1)[:, None, :]
    turned = jnp.concatenate([-values[..., half_dim:], values[..., :half_dim]], axis=-1)
    return values * jnp.cos(angles) + turned * jnp.sin(angles)


def project(inputs, weight):
    return jnp.dot(
        inputs,
        lax.all_gather(weight, "fsdp", axis=0, tiled=True),
        preferred_element_type=jnp.float32,
    )


def general_body(byte_ids, byte_table, w_conv, w_qkv, w_out, norm_gain, teacher, align):
    seq_bytes = byte_ids.shape[1]
    lat_rows = seq_bytes // KW
    query_width = HQ * HD
    key_width = HK * HD
    one_hot = (
        byte_ids[0][:, None] == jnp.arange(byte_table.shape[0], dtype=jnp.int32)[None, :]
    ).astype(jnp.bfloat16)
    embedded = jnp.dot(one_hot, byte_table, preferred_element_type=jnp.float32).astype(jnp.bfloat16)
    stacked = embedded.reshape(lat_rows, KW * byte_table.shape[1])
    latent = project(stacked, w_conv).astype(jnp.bfloat16)
    latent_wide = latent.astype(jnp.float32)
    scale_rows = lax.rsqrt(jnp.mean(latent_wide * latent_wide, axis=1, keepdims=True) + norm_eps)
    normed = (latent_wide * scale_rows * norm_gain.astype(jnp.float32)[None, :]).astype(
        jnp.bfloat16
    )
    projected = project(normed, w_qkv)
    ctx_index = lax.axis_index("ctx")
    positions = ctx_index * lat_rows + jnp.arange(lat_rows, dtype=jnp.int32)
    queries = rotate(projected[:, :query_width].reshape(lat_rows, HQ, HD), positions).astype(
        jnp.bfloat16
    )
    key_rows = rotate(
        projected[:, query_width : query_width + key_width].reshape(lat_rows, HK, HD), positions
    )
    key_rows = key_rows.astype(jnp.bfloat16).reshape(lat_rows, key_width)
    value_rows = projected[:, query_width + key_width :].astype(jnp.bfloat16)
    grouped = queries.reshape(lat_rows, HK, HQ // HK, HD)
    start_state = (
        jnp.full((HK, HQ // HK, lat_rows), masked_score, jnp.float32),
        jnp.zeros((HK, HQ // HK, lat_rows), jnp.float32),
        jnp.zeros((HK, HQ // HK, lat_rows, HD), jnp.float32),
    )
    key_all = lax.all_gather(key_rows, "ctx", axis=0, tiled=True)
    value_all = lax.all_gather(value_rows, "ctx", axis=0, tiled=True)
    blocks = key_all.shape[0] // lat_rows
    key_blocks = key_all.reshape(blocks, lat_rows, HK, HD)
    value_blocks = value_all.reshape(blocks, lat_rows, HK, HD)
    block_starts = lat_rows * jnp.arange(blocks, dtype=jnp.int32)

    def one_block(partial_value, block_data):
        key_block, value_block, key_start = block_data
        row_top, row_mass, weighted = partial_value
        scores = (
            jnp.einsum("qkgd,skd->kgqs", grouped, key_block, preferred_element_type=jnp.float32)
            * score_scale
        )
        key_pos = key_start + jnp.arange(lat_rows, dtype=jnp.int32)
        allowed = key_pos[None, :] <= positions[:, None]
        scores = jnp.where(allowed[None, None], scores, masked_score)
        new_top = jnp.maximum(row_top, jnp.max(scores, axis=-1))
        weights = jnp.exp(scores - new_top[..., None])
        shrink = jnp.exp(row_top - new_top)
        row_mass = row_mass * shrink + jnp.sum(weights, axis=-1)
        weighted = weighted * shrink[..., None] + jnp.einsum(
            "kgqs,skd->kgqd",
            weights.astype(jnp.bfloat16),
            value_block,
            preferred_element_type=jnp.float32,
        )
        return ((new_top, row_mass, weighted), None)

    result, unused = lax.scan(one_block, start_state, (key_blocks, value_blocks, block_starts))
    final_top, final_mass, final_sum = result
    attended = final_sum / final_mass[..., None]
    attended = jnp.transpose(attended, (2, 0, 1, 3)).reshape(lat_rows, HQ * HD).astype(jnp.bfloat16)
    branch = project(attended, w_out)
    hidden_out = (latent_wide + branch).astype(jnp.bfloat16)
    local_rows = align[0] - ctx_index * lat_rows
    picked = jnp.take(hidden_out, local_rows, axis=0)
    difference = picked.astype(jnp.float32) - teacher[0].astype(jnp.float32)
    token_loss = jnp.mean(difference * difference, axis=1)
    return (hidden_out[None], token_loss[None])


def rope_tables(length):
    half = HD // 2
    frequency = np.float32(theta_base) ** (-np.arange(half, dtype=np.float32) * np.float32(2.0 / HD))
    angles = np.arange(length, dtype=np.float32)[:, None] * frequency[None, :]
    angles = angles.astype(np.float64)
    cos, sin = np.cos(angles).astype(np.float32), np.sin(angles).astype(np.float32)
    return np.concatenate([cos] * 4, axis=1), np.concatenate([-sin, sin] * 2, axis=1)


def turn(x, cos, sin):
    half = HD // 2
    lane = lax.broadcasted_iota(jnp.int32, x.shape, 1)
    low = (lane & half) == 0
    swapped = jnp.where(low, pltpu.roll(x, 128 - half, axis=1), pltpu.roll(x, half, axis=1))
    return x * cos + swapped * sin


def part_kernel(where_ref, qkv_ref, part_ref):
    side = where_ref[2] % 2
    start = 0
    for width in (HQ * HD, HK * HD, HK * HD):
        own = width // 2
        part_ref[:, start // 2 : start // 2 + own] = qkv_ref[
            :, pl.ds(pl.multiple_of(start + side * own, own), own)
        ]
        start += width


def table_kernel(where_ref, bytes_ref, conv_ref, total_ref, part_ref, align_ref, out_ref, both_ref, align_out):
    align_out[...] = align_ref[...]
    core = where_ref[1]
    taps_in = conv_ref.shape[0]
    half = total_ref.shape[0]
    rows = pl.ds(pl.multiple_of(core * half, half), half)
    mates = bytes_ref[rows, pl.ds(pl.multiple_of((1 - core) * taps_in, taps_in), taps_in)]
    total = total_ref[...] + jnp.dot(mates, conv_ref[...], preferred_element_type=jnp.float32)
    out_ref[...] = total.astype(jnp.bfloat16)
    both_ref[:, : total.shape[1]] = total.astype(jnp.bfloat16)
    both_ref[:, total.shape[1] :] = part_ref[...]


def ordered(chip, core, pieces):
    own, near, mate_own, mate_near = pieces
    depth = own.shape[0]
    for j, (mine, mates) in enumerate(zip((own,) + near, (mate_own,) + mate_near)):
        base = (chip ^ j) * 2
        for which, piece in ((core, mine), (1 - core, mates)):
            yield pl.ds(pl.multiple_of((base + which) * depth, depth), depth), piece


def attend(queries, key_slots, allowed, k_s, v_s, att_ref):
    heads = HQ // 2

    def one_head(h):
        query = queries(h)
        group = h // GROUP
        scores = [
            lax.dot_general(
                k_s[slot, group], query, (((1,), (1,)), ((), ())), preferred_element_type=jnp.float32
            )
            for slot in key_slots
        ]
        scores[-1] = jnp.where(allowed, scores[-1], masked_score)
        top = functools.reduce(jnp.maximum, [jnp.max(s, axis=0, keepdims=True) for s in scores])
        total = None
        for slot, s in zip(key_slots, scores):
            probs = jnp.exp(s - top).astype(jnp.bfloat16)
            term = jnp.dot(v_s[slot, group], probs, preferred_element_type=jnp.float32)
            total = term if total is None else total + term
        return total[:HD] / total[HD : HD + 1]

    for pair in range(heads // 2):
        result = jnp.concatenate([one_head(2 * pair), one_head(2 * pair + 1)], axis=0)
        att_ref[:, pair * 2 * HD : (pair + 1) * 2 * HD] = jnp.transpose(result).astype(jnp.bfloat16)


def causal(rows):
    return lax.broadcasted_iota(jnp.int32, (rows, rows), 0) <= lax.broadcasted_iota(
        jnp.int32, (rows, rows), 1
    )


def key_variants(ctx, which):
    for block in range(2):
        now = tuple(range(2, 3 + block))
        yield (which == block) & (ctx < 2), block, now
        yield (which == block) & (ctx >= 2), block, (0, 1) + now


def lift_kernel(
    where_ref, ids_refs, own_t, near_t, mate_own_t, mate_near_t, own_w, near_w, mate_own_w, mate_near_w,
    gain_ref, cos_ref, sin_ref, att_ref, query_ref, k_s, v_s, lat_ref,
    table_s, weight_s, ids_s, lat_s, q_s,
):
    chip, core, ctx = where_ref[0], where_ref[1], where_ref[2]
    side, upper = ctx % 2, ctx // 2
    rows, features = lat_ref.shape
    q_width, k_width = HQ * HD // 2, HK * HD // 2
    for span, piece in ordered(chip, core, (own_t, near_t, mate_own_t, mate_near_t)):
        table_s[span, :] = piece[:, :features]
    near_w, mate_near_w = near_w + (near_t[-1],), mate_near_w + (mate_near_t[-1],)
    for span, piece in ordered(chip, core, (own_w, near_w, mate_own_w, mate_near_w)):
        weight_s[span, :] = piece[:, -weight_s.shape[1] :]
    own_ids, pair_ids, past_ids, cross_ids = ids_refs
    ids_s[side] = past_ids[...]
    ids_s[1 - side] = cross_ids[...]
    ids_s[2 + side] = own_ids[...]
    ids_s[3 - side] = pair_ids[...]
    gain = gain_ref[...].astype(jnp.float32)
    v_s[:, :, HD:, :] = jnp.ones(v_s.shape[:2] + (v_s.shape[2] - HD, rows), jnp.bfloat16)

    def lift(slot):
        ids = jnp.transpose(ids_s[slot])
        byte = lax.broadcasted_iota(jnp.int32, (rows, VOCAB), 1)
        one_hot = jnp.concatenate(
            [(ids[:, k : k + 1] == byte).astype(jnp.float32).astype(jnp.bfloat16) for k in range(KW)], axis=1
        )
        latent = jnp.dot(one_hot, table_s[...], preferred_element_type=jnp.float32).astype(jnp.bfloat16)
        wide = latent.astype(jnp.float32)
        scale = lax.rsqrt(jnp.mean(wide * wide, axis=1, keepdims=True) + norm_eps)
        normed = (wide * scale * gain).astype(jnp.bfloat16)
        block = slot if slot < 2 else 2 * upper + slot - 2
        cos, sin = cos_ref[block], sin_ref[block]
        if slot >= 2:
            lat_s[slot - 2] = latent
            asked = jnp.dot(normed, weight_s[:, :q_width], preferred_element_type=jnp.float32)
            for pair in range(q_width // 128):
                turned = turn(asked[:, pair * 128 : (pair + 1) * 128], cos, sin)
                turned = (turned * score_scale).astype(jnp.bfloat16)
                q_s[slot - 2, 2 * pair] = turned[:, :HD]
                q_s[slot - 2, 2 * pair + 1] = turned[:, HD:]
        kept = jnp.dot(normed, weight_s[:, q_width:], preferred_element_type=jnp.float32)
        keys = turn(kept[:, :k_width], cos, sin).astype(jnp.bfloat16)
        values = jnp.transpose(kept[:, k_width:]).astype(jnp.bfloat16)
        for group in range(2):
            k_s[slot, group] = keys[:, group * HD : (group + 1) * HD]
            v_s[slot, group, :HD, :] = values[group * HD : (group + 1) * HD]

    @pl.when(upper == 1)
    def _():
        lift(0)
        lift(1)

    lift(2)
    lift(3)
    lat_ref[...] = lat_s[side]
    query_ref[...] = q_s[side]
    allowed = causal(rows)
    other = 1 - side
    for condition, block, slots in key_variants(ctx, other):

        @pl.when(condition)
        def _(block=block, slots=slots):
            attend(lambda h: q_s[block, h], slots, allowed, k_s, v_s, att_ref)


def own_kernel(where_ref, query_ref, k_ref, v_ref, att_ref):
    ctx = where_ref[2]
    allowed = causal(att_ref.shape[0])
    for condition, block, slots in key_variants(ctx, ctx % 2):

        @pl.when(condition)
        def _(slots=slots):
            attend(lambda h: query_ref[h], slots, allowed, k_ref, v_ref, att_ref)


def out_kernel(
    where_ref, own_att, mate_att, own, near, mate_own, mate_near, lat_ref, teacher_ref, align_ref,
    hidden_ref, loss_ref, att_s, weight_s,
):
    chip, core, ctx = where_ref[0], where_ref[1], where_ref[2]
    side = ctx % 2
    rows, width = lat_ref.shape
    part = own_att.shape[1]
    for span, piece in ordered(chip, core, (own, near, mate_own, mate_near)):
        weight_s[span, :] = piece[...]
    att_s[:, pl.ds(pl.multiple_of(side * part, part), part)] = own_att[...]
    att_s[:, pl.ds(pl.multiple_of((1 - side) * part, part), part)] = mate_att[...]
    branch = jnp.dot(att_s[...], weight_s[...], preferred_element_type=jnp.float32)
    hidden = (lat_ref[...].astype(jnp.float32) + branch).astype(jnp.bfloat16)
    hidden_ref[...] = hidden
    source = lax.broadcasted_iota(jnp.int32, (rows, rows), 0) + ctx * rows
    chosen = (source == align_ref[...]).astype(jnp.float32).astype(jnp.bfloat16)
    picked = lax.dot_general(
        chosen, hidden, (((0,), (0,)), ((), ())), preferred_element_type=jnp.float32
    )
    difference = picked - teacher_ref[...].astype(jnp.float32)
    square = difference * difference
    lanes = square[:, :128]
    for start in range(128, width, 128):
        lanes = lanes + square[:, start : start + 128]
    loss_ref[...] = jnp.sum(jnp.transpose(lanes), axis=0, keepdims=True) * (1.0 / width)


VMEM = pl.BlockSpec(memory_space=pltpu.VMEM)
SMEM = pl.BlockSpec(memory_space=pltpu.SMEM)
MIB = 1024 * 1024


def call(kernel, name, mib, flops, in_specs, outs, scratch=()):
    return pl.pallas_call(
        kernel,
        out_shape=tuple(jax.ShapeDtypeStruct(shape, dtype) for shape, dtype in outs),
        in_specs=in_specs,
        out_specs=(VMEM,) * len(outs),
        scratch_shapes=[pltpu.VMEM(shape, dtype) for shape, dtype in scratch],
        compiler_params=pltpu.CompilerParams(vmem_limit_bytes=mib * MIB),
        cost_estimate=pl.CostEstimate(flops=flops, bytes_accessed=4 * MIB, transcendentals=0),
        name=name,
    )


def head_body(sizes, byte_ids, byte_table, w_conv, w_qkv, w_out, norm_gain, teacher, align):
    n_fsdp, n_ctx = sizes
    me, ctx = lax.axis_index("fsdp"), lax.axis_index("ctx")
    chip, core = me // 2, me % 2
    rows = byte_ids.shape[1] // KW
    features = w_conv.shape[1]
    q_width = HQ * HD // 2
    part_width = w_qkv.shape[1] // 2
    half = VOCAB // 2
    bf16, f32 = jnp.bfloat16, jnp.float32
    where = jnp.stack([chip, core, ctx]).astype(jnp.int32)

    def swap(x, j):
        return lax.ppermute(x, "fsdp", [(d, d ^ j) for d in range(n_fsdp)])

    def along(x, pairs):
        return lax.ppermute(x, "ctx", pairs)

    def to_near(x):
        return tuple(swap(x, 2 * j) for j in range(1, n_fsdp // 2))

    def to_mate(x, near):
        return x, near, swap(x, 1), tuple(swap(piece, 1) for piece in near)

    beside = [(z, z ^ 1) for z in range(n_ctx)]

    mate_conv = swap(w_conv, 1)
    (part,) = call(
        part_kernel, "qkv_part", 4, 10**8, [SMEM, VMEM], [((w_qkv.shape[0], part_width), bf16)]
    )(where, w_qkv)
    near_w = tuple(swap(part, 2 * j) for j in (1, 2))

    taps_in = w_conv.shape[0]
    mine = lax.dynamic_slice(byte_table, (core * half, core * taps_in), (half, taps_in))
    total = jnp.dot(mine, w_conv, preferred_element_type=f32)
    own_t, both, align = call(
        table_kernel, "tap_table", 8, 10**8, [SMEM] + [VMEM] * 5,
        [((half, features), bf16), ((half, features + part_width), bf16), (align.shape, jnp.int32)],
    )(where, byte_table, mate_conv, total, part, align)
    (own_t, both), near_w = lax.optimization_barrier(((own_t, both), near_w))
    near_t = (swap(own_t, 2), swap(own_t, 4), swap(both, 6))
    ids = jnp.transpose(byte_ids[0].reshape(rows, KW))
    ids = jnp.pad(ids, ((0, 8 - KW), (0, 0)))
    ids, unused = lax.optimization_barrier((ids, own_t))
    ids_all = (
        ids,
        along(ids, beside),
        along(ids, [(0, 2), (1, 3)]),
        along(ids, [(0, 3), (1, 2)]),
    )
    last, ids_all = lax.optimization_barrier((near_t[-1], ids_all))
    near_t = near_t[:-1] + (last,)
    t_pieces, w_pieces = to_mate(own_t, near_t), to_mate(part, near_w)
    out_own, unused = lax.optimization_barrier((w_out, near_t))
    out_near = to_near(out_own)

    cos, sin = (jnp.asarray(t.reshape(n_ctx, rows, 128)) for t in rope_tables(rows * n_ctx))
    near_specs = (VMEM,) * (n_fsdp // 2 - 1)
    piece_specs = [VMEM, near_specs, VMEM, near_specs]
    att_shape = ((rows, q_width), bf16)
    att_mate, query, keys, values, latent = call(
        lift_kernel, "lift", 18, 5 * 10**9,
        [SMEM, (VMEM,) * 4] + piece_specs + [VMEM, (VMEM,) * 2] * 2 + [VMEM, VMEM, VMEM],
        [
            att_shape,
            ((HQ // 2, rows, HD), bf16),
            ((4, 2, rows, HD), bf16),
            ((4, 2, HD + 16, rows), bf16),
            ((rows, features), bf16),
        ],
        [
            ((KW * VOCAB, features), bf16),
            ((features, part_width), bf16),
            ((4, 8, rows), jnp.int32),
            ((2, rows, features), bf16),
            ((2, HQ // 2, rows, HD), bf16),
        ],
    )(where, ids_all, *t_pieces, *w_pieces, norm_gain[None], cos, sin)

    att_mate, out_near = lax.optimization_barrier((att_mate, out_near))
    att_back = along(att_mate, beside)
    (att_own,) = call(
        own_kernel, "own_block", 12, 3 * 10**9, [SMEM, VMEM, VMEM, VMEM], [att_shape]
    )(where, query, keys, values)
    hidden, loss = call(
        out_kernel, "project_out", 12, 10**9,
        [SMEM, VMEM, VMEM] + piece_specs + [VMEM, VMEM, VMEM],
        [((rows, features), bf16), ((1, rows), f32)],
        [((rows, features), bf16), ((features, features), bf16)],
    )(where, att_own, att_back, *to_mate(out_own, out_near), latent, teacher[0], align)
    return hidden[None], loss


def solution(mesh):
    in_specs = (
        P("fsdp", "ctx"),
        P(),
        P("fsdp", None),
        P("fsdp", None),
        P("fsdp", None),
        P(),
        P("fsdp", "ctx", None),
        P("fsdp", "ctx"),
    )
    out_specs = (P("fsdp", "ctx", None), P("fsdp", "ctx"))
    sizes = (mesh.shape["fsdp"], mesh.shape["ctx"])
    body = functools.partial(head_body, sizes) if sizes == (2 * KW, HK) else general_body
    return jax.shard_map(body, mesh=mesh, in_specs=in_specs, out_specs=out_specs, check_vma=False)
```

```python
import functools
import math

import jax
import jax.numpy as jnp
import numpy as np
from jax import lax
from jax.experimental import pallas as pl
from jax.experimental.pallas import tpu as pltpu
from jax.sharding import PartitionSpec as P

KW = 4
HQ = 16
HK = 4
HD = 64
GROUP = HQ // HK
VOCAB = 256

theta_base = 500000.0
norm_eps = 1e-05
masked_score = -1e30
score_scale = 1.0 / math.sqrt(HD)


def rotate(values, positions):
    half_dim = values.shape[-1] // 2
    frequency = theta_base ** (-jnp.arange(half_dim, dtype=jnp.float32) * 2.0 / values.shape[-1])
    angles = positions.astype(jnp.float32)[:, None] * frequency[None, :]
    angles = jnp.concatenate([angles, angles], axis=-1)[:, None, :]
    turned = jnp.concatenate([-values[..., half_dim:], values[..., :half_dim]], axis=-1)
    return values * jnp.cos(angles) + turned * jnp.sin(angles)


def project(inputs, weight):
    return jnp.dot(
        inputs,
        lax.all_gather(weight, "fsdp", axis=0, tiled=True),
        preferred_element_type=jnp.float32,
    )


def general_body(byte_ids, byte_table, w_conv, w_qkv, w_out, norm_gain, teacher, align):
    seq_bytes = byte_ids.shape[1]
    lat_rows = seq_bytes // KW
    query_width = HQ * HD
    key_width = HK * HD
    one_hot = (
        byte_ids[0][:, None] == jnp.arange(byte_table.shape[0], dtype=jnp.int32)[None, :]
    ).astype(jnp.bfloat16)
    embedded = jnp.dot(one_hot, byte_table, preferred_element_type=jnp.float32).astype(jnp.bfloat16)
    stacked = embedded.reshape(lat_rows, KW * byte_table.shape[1])
    latent = project(stacked, w_conv).astype(jnp.bfloat16)
    latent_wide = latent.astype(jnp.float32)
    scale_rows = lax.rsqrt(jnp.mean(latent_wide * latent_wide, axis=1, keepdims=True) + norm_eps)
    normed = (latent_wide * scale_rows * norm_gain.astype(jnp.float32)[None, :]).astype(
        jnp.bfloat16
    )
    projected = project(normed, w_qkv)
    ctx_index = lax.axis_index("ctx")
    positions = ctx_index * lat_rows + jnp.arange(lat_rows, dtype=jnp.int32)
    queries = rotate(projected[:, :query_width].reshape(lat_rows, HQ, HD), positions).astype(
        jnp.bfloat16
    )
    key_rows = rotate(
        projected[:, query_width : query_width + key_width].reshape(lat_rows, HK, HD), positions
    )
    key_rows = key_rows.astype(jnp.bfloat16).reshape(lat_rows, key_width)
    value_rows = projected[:, query_width + key_width :].astype(jnp.bfloat16)
    grouped = queries.reshape(lat_rows, HK, HQ // HK, HD)
    start_state = (
        jnp.full((HK, HQ // HK, lat_rows), masked_score, jnp.float32),
        jnp.zeros((HK, HQ // HK, lat_rows), jnp.float32),
        jnp.zeros((HK, HQ // HK, lat_rows, HD), jnp.float32),
    )
    key_all = lax.all_gather(key_rows, "ctx", axis=0, tiled=True)
    value_all = lax.all_gather(value_rows, "ctx", axis=0, tiled=True)
    blocks = key_all.shape[0] // lat_rows
    key_blocks = key_all.reshape(blocks, lat_rows, HK, HD)
    value_blocks = value_all.reshape(blocks, lat_rows, HK, HD)
    block_starts = lat_rows * jnp.arange(blocks, dtype=jnp.int32)

    def one_block(partial_value, block_data):
        key_block, value_block, key_start = block_data
        row_top, row_mass, weighted = partial_value
        scores = (
            jnp.einsum("qkgd,skd->kgqs", grouped, key_block, preferred_element_type=jnp.float32)
            * score_scale
        )
        key_pos = key_start + jnp.arange(lat_rows, dtype=jnp.int32)
        allowed = key_pos[None, :] <= positions[:, None]
        scores = jnp.where(allowed[None, None], scores, masked_score)
        new_top = jnp.maximum(row_top, jnp.max(scores, axis=-1))
        weights = jnp.exp(scores - new_top[..., None])
        shrink = jnp.exp(row_top - new_top)
        row_mass = row_mass * shrink + jnp.sum(weights, axis=-1)
        weighted = weighted * shrink[..., None] + jnp.einsum(
            "kgqs,skd->kgqd",
            weights.astype(jnp.bfloat16),
            value_block,
            preferred_element_type=jnp.float32,
        )
        return ((new_top, row_mass, weighted), None)

    result, unused = lax.scan(one_block, start_state, (key_blocks, value_blocks, block_starts))
    final_top, final_mass, final_sum = result
    attended = final_sum / final_mass[..., None]
    attended = jnp.transpose(attended, (2, 0, 1, 3)).reshape(lat_rows, HQ * HD).astype(jnp.bfloat16)
    branch = project(attended, w_out)
    hidden_out = (latent_wide + branch).astype(jnp.bfloat16)
    local_rows = align[0] - ctx_index * lat_rows
    picked = jnp.take(hidden_out, local_rows, axis=0)
    difference = picked.astype(jnp.float32) - teacher[0].astype(jnp.float32)
    token_loss = jnp.mean(difference * difference, axis=1)
    return (hidden_out[None], token_loss[None])


def rope_tables(blocks, rows):
    half = HD // 2
    frequency = np.float32(theta_base) ** (-np.arange(half, dtype=np.float32) * np.float32(2.0 / HD))
    places = [np.arange(rows), np.arange(blocks) * rows]
    angles = [np.concatenate([p[:, None] * frequency[None, :].astype(np.float64)] * 4, axis=1) for p in places]
    parts = [f(angles[0]) for f in (np.cos, np.sin)] + [f(angles[1]) for f in (np.cos, np.sin)]
    return np.concatenate(parts, axis=0).astype(np.float32)


def rope_at(rope_ref, rows, block):
    blocks = (rope_ref.shape[0] - 2 * rows) // 2
    cos, sin = rope_ref[:rows, :], rope_ref[rows : 2 * rows, :]
    cos_start = rope_ref[pl.ds(2 * rows + block, 1), :]
    sin_start = rope_ref[pl.ds(2 * rows + blocks + block, 1), :]
    lane = lax.broadcasted_iota(jnp.int32, (1, 128), 1)
    sign = jnp.where((lane & (HD // 2)) == 0, -1.0, 1.0)
    return (
        cos * cos_start - sin * sin_start,
        sin * (cos_start * sign) + cos * (sin_start * sign),
    )


def turn(x, cos, sin):
    half = HD // 2
    lane = lax.broadcasted_iota(jnp.int32, x.shape, 1)
    low = (lane & half) == 0
    swapped = jnp.where(low, pltpu.roll(x, 128 - half, axis=1), pltpu.roll(x, half, axis=1))
    return x * cos + swapped * sin


def part_kernel(where_ref, qkv_ref, part_ref):
    side = where_ref[2] % 2
    start = 0
    for width in (HQ * HD, HK * HD, HK * HD):
        own = width // 2
        part_ref[:, start // 2 : start // 2 + own] = qkv_ref[
            :, pl.ds(pl.multiple_of(start + side * own, own), own)
        ]
        start += width


def table_kernel(where_ref, bytes_ref, conv_ref, total_ref, align_ref, rope_ref, out_ref, align_out, rope_out):
    align_out[...] = align_ref[...]
    rope_out[...] = rope_ref[...]
    core = where_ref[1]
    taps_in = conv_ref.shape[0]
    half = total_ref.shape[0]
    rows = pl.ds(pl.multiple_of(core * half, half), half)
    mates = bytes_ref[rows, pl.ds(pl.multiple_of((1 - core) * taps_in, taps_in), taps_in)]
    total = total_ref[...] + jnp.dot(mates, conv_ref[...], preferred_element_type=jnp.float32)
    out_ref[...] = total.astype(jnp.bfloat16)


def ordered(chip, core, pieces):
    own, near, mate_own, mate_near = pieces
    depth = own.shape[0]
    for j, (mine, mates) in enumerate(zip((own,) + near, (mate_own,) + mate_near)):
        base = (chip ^ j) * 2
        for which, piece in ((core, mine), (1 - core, mates)):
            yield pl.ds(pl.multiple_of((base + which) * depth, depth), depth), piece


def attend(queries, slots, allowed, k_s, v_s, att_ref):
    heads = HQ // 2
    rows = att_ref.shape[0]
    keys = slice(slots[0] * rows, (slots[-1] + 1) * rows)

    def score(h):
        scores = lax.dot_general(
            k_s[h // GROUP, keys, :], queries(h), (((1,), (1,)), ((), ())), preferred_element_type=jnp.float32
        )
        last = jnp.where(allowed, scores[-rows:], masked_score)
        return last if len(slots) == 1 else jnp.concatenate([scores[:-rows], last], axis=0)

    coming, results = score(0), []
    for h in range(heads):
        scores = coming
        if h + 1 < heads:
            coming = score(h + 1)
        probs = jnp.exp(scores - jnp.max(scores, axis=0, keepdims=True)).astype(jnp.bfloat16)
        total = jnp.dot(v_s[h // GROUP, :, keys], probs, preferred_element_type=jnp.float32)
        results.append(total[:HD] / total[HD : HD + 1])
        if h % 2 == 1:
            pair = jnp.transpose(jnp.concatenate(results[-2:], axis=0))
            att_ref[:, (h - 1) * HD : (h + 1) * HD] = pair.astype(jnp.bfloat16)


def causal(rows):
    return lax.broadcasted_iota(jnp.int32, (rows, rows), 0) <= lax.broadcasted_iota(
        jnp.int32, (rows, rows), 1
    )


def key_variants(ctx, which):
    for block in range(2):
        now = tuple(range(2, 3 + block))
        yield (which == block) & (ctx < 2), block, now
        yield (which == block) & (ctx >= 2), block, (0, 1) + now


def lift_kernel(
    where_ref, ids_refs, own_t, near_t, mate_own_t, mate_near_t, own_w, near_w, mate_own_w, mate_near_w,
    gain_ref, rope_ref, att_ref, query_ref, k_s, v_s, lat_ref,
    table_s, weight_s, ids_s, lat_s, q_s,
):
    chip, core, ctx = where_ref[0], where_ref[1], where_ref[2]
    side, upper = ctx % 2, ctx // 2
    rows, features = lat_ref.shape
    q_width, k_width = HQ * HD // 2, HK * HD // 2
    for span, piece in ordered(chip, core, (own_t, near_t, mate_own_t, mate_near_t)):
        table_s[span, :] = piece[...]
    for span, piece in ordered(chip, core, (own_w, near_w, mate_own_w, mate_near_w)):
        weight_s[span, :] = piece[...]
    own_ids, pair_ids, past_ids, cross_ids = ids_refs
    ids_s[side] = past_ids[...]
    ids_s[1 - side] = cross_ids[...]
    ids_s[2 + side] = own_ids[...]
    ids_s[3 - side] = pair_ids[...]
    gain = gain_ref[...].astype(jnp.float32)
    v_s[:, HD:, :] = jnp.ones((v_s.shape[0], v_s.shape[1] - HD, v_s.shape[2]), jnp.bfloat16)

    def lift(slot):
        ids = jnp.transpose(ids_s[slot])
        byte = lax.broadcasted_iota(jnp.int32, (rows, VOCAB), 1)
        one_hot = jnp.concatenate(
            [(ids[:, k : k + 1] == byte).astype(jnp.float32).astype(jnp.bfloat16) for k in range(KW)], axis=1
        )
        latent = jnp.dot(one_hot, table_s[...], preferred_element_type=jnp.float32).astype(jnp.bfloat16)
        wide = latent.astype(jnp.float32)
        scale = lax.rsqrt(jnp.mean(wide * wide, axis=1, keepdims=True) + norm_eps)
        normed = (wide * scale * gain).astype(jnp.bfloat16)
        block = slot if slot < 2 else 2 * upper + slot - 2
        cos, sin = rope_at(rope_ref, rows, block)
        if slot >= 2:
            lat_s[slot - 2] = latent
            asked = jnp.dot(normed, weight_s[:, :q_width], preferred_element_type=jnp.float32)
            for pair in range(q_width // 128):
                turned = turn(asked[:, pair * 128 : (pair + 1) * 128], cos, sin)
                turned = (turned * score_scale).astype(jnp.bfloat16)
                q_s[slot - 2, 2 * pair] = turned[:, :HD]
                q_s[slot - 2, 2 * pair + 1] = turned[:, HD:]
        kept = jnp.dot(normed, weight_s[:, q_width:], preferred_element_type=jnp.float32)
        keys = turn(kept[:, :k_width], cos, sin).astype(jnp.bfloat16)
        values = jnp.transpose(kept[:, k_width:]).astype(jnp.bfloat16)
        for group in range(2):
            k_s[group, slot * rows : (slot + 1) * rows, :] = keys[:, group * HD : (group + 1) * HD]
            v_s[group, :HD, slot * rows : (slot + 1) * rows] = values[group * HD : (group + 1) * HD]

    @pl.when(upper == 1)
    def _():
        lift(0)
        lift(1)

    lift(2)
    lift(3)
    lat_ref[...] = lat_s[side]
    query_ref[...] = q_s[side]
    allowed = causal(rows)
    other = 1 - side
    for condition, block, slots in key_variants(ctx, other):

        @pl.when(condition)
        def _(block=block, slots=slots):
            attend(lambda h: q_s[block, h], slots, allowed, k_s, v_s, att_ref)


def own_kernel(where_ref, query_ref, k_ref, v_ref, att_ref):
    ctx = where_ref[2]
    allowed = causal(att_ref.shape[0])
    for condition, block, slots in key_variants(ctx, ctx % 2):

        @pl.when(condition)
        def _(slots=slots):
            attend(lambda h: query_ref[h], slots, allowed, k_ref, v_ref, att_ref)


def out_kernel(
    where_ref, own_att, mate_att, own, near, mate_own, mate_near, lat_ref, teacher_ref, align_ref,
    hidden_ref, loss_ref, att_s, weight_s,
):
    chip, core, ctx = where_ref[0], where_ref[1], where_ref[2]
    side = ctx % 2
    rows, width = lat_ref.shape
    part = own_att.shape[1]
    for span, piece in ordered(chip, core, (own, near, mate_own, mate_near)):
        weight_s[span, :] = piece[...]
    att_s[:, pl.ds(pl.multiple_of(side * part, part), part)] = own_att[...]
    att_s[:, pl.ds(pl.multiple_of((1 - side) * part, part), part)] = mate_att[...]
    branch = jnp.dot(att_s[...], weight_s[...], preferred_element_type=jnp.float32)
    hidden = (lat_ref[...].astype(jnp.float32) + branch).astype(jnp.bfloat16)
    hidden_ref[...] = hidden
    source = lax.broadcasted_iota(jnp.int32, (rows, rows), 0) + ctx * rows
    chosen = (source == align_ref[...]).astype(jnp.float32).astype(jnp.bfloat16)
    picked = lax.dot_general(
        chosen, hidden, (((0,), (0,)), ((), ())), preferred_element_type=jnp.float32
    )
    difference = picked - teacher_ref[...].astype(jnp.float32)
    square = difference * difference
    lanes = square[:, :128]
    for start in range(128, width, 128):
        lanes = lanes + square[:, start : start + 128]
    loss_ref[...] = jnp.sum(jnp.transpose(lanes), axis=0, keepdims=True) * (1.0 / width)


VMEM = pl.BlockSpec(memory_space=pltpu.VMEM)
SMEM = pl.BlockSpec(memory_space=pltpu.SMEM)
MIB = 1024 * 1024


def call(kernel, name, mib, flops, in_specs, outs, scratch=()):
    return pl.pallas_call(
        kernel,
        out_shape=tuple(jax.ShapeDtypeStruct(shape, dtype) for shape, dtype in outs),
        in_specs=in_specs,
        out_specs=(VMEM,) * len(outs),
        scratch_shapes=[pltpu.VMEM(shape, dtype) for shape, dtype in scratch],
        compiler_params=pltpu.CompilerParams(vmem_limit_bytes=mib * MIB),
        cost_estimate=pl.CostEstimate(flops=flops, bytes_accessed=4 * MIB, transcendentals=0),
        name=name,
    )


def head_body(sizes, byte_ids, byte_table, w_conv, w_qkv, w_out, norm_gain, teacher, align):
    n_fsdp, n_ctx = sizes
    me, ctx = lax.axis_index("fsdp"), lax.axis_index("ctx")
    chip, core = me // 2, me % 2
    rows = byte_ids.shape[1] // KW
    features = w_conv.shape[1]
    q_width = HQ * HD // 2
    part_width = w_qkv.shape[1] // 2
    half = VOCAB // 2
    bf16, f32 = jnp.bfloat16, jnp.float32
    where = jnp.stack([chip, core, ctx]).astype(jnp.int32)

    def swap(x, j):
        return lax.ppermute(x, "fsdp", [(d, d ^ j) for d in range(n_fsdp)])

    def along(x, pairs):
        return lax.ppermute(x, "ctx", pairs)

    def to_near(x):
        return tuple(swap(x, 2 * j) for j in range(1, n_fsdp // 2))

    def to_mate(x, near):
        return x, near, swap(x, 1), tuple(swap(piece, 1) for piece in near)

    beside = [(z, z ^ 1) for z in range(n_ctx)]

    mate_conv = swap(w_conv, 1)
    (part,) = call(
        part_kernel, "qkv_part", 4, 10**8, [SMEM, VMEM], [((w_qkv.shape[0], part_width), bf16)]
    )(where, w_qkv)
    near_w = to_near(part)

    taps_in = w_conv.shape[0]
    mine = lax.dynamic_slice(byte_table, (core * half, core * taps_in), (half, taps_in))
    total = jnp.dot(mine, w_conv, preferred_element_type=f32)
    rope = jnp.asarray(rope_tables(n_ctx, rows))
    own_t, align, rope = call(
        table_kernel, "tap_table", 8, 10**8, [SMEM] + [VMEM] * 5,
        [((half, features), bf16), (align.shape, jnp.int32), (rope.shape, f32)],
    )(where, byte_table, mate_conv, total, align, rope)
    own_t, first = lax.optimization_barrier((own_t, near_w[0]))
    near_w = (first,) + near_w[1:]
    near_t = to_near(own_t)
    ids = jnp.transpose(byte_ids[0].reshape(rows, KW))
    ids = jnp.pad(ids, ((0, 8 - KW), (0, 0)))
    ids, unused = lax.optimization_barrier((ids, own_t))
    ids_all = (
        ids,
        along(ids, beside),
        along(ids, [(0, 2), (1, 3)]),
        along(ids, [(0, 3), (1, 2)]),
    )
    last, ids_all = lax.optimization_barrier((near_t[-1], ids_all))
    near_t = near_t[:-1] + (last,)
    t_pieces, w_pieces = to_mate(own_t, near_t), to_mate(part, near_w)
    out_own, unused = lax.optimization_barrier((w_out, near_t))
    out_near = to_near(out_own)

    near_specs = (VMEM,) * (n_fsdp // 2 - 1)
    piece_specs = [VMEM, near_specs, VMEM, near_specs]
    att_shape = ((rows, q_width), bf16)
    att_mate, query, keys, values, latent = call(
        lift_kernel, "lift", 18, 5 * 10**9,
        [SMEM, (VMEM,) * 4] + piece_specs + piece_specs + [VMEM, VMEM],
        [
            att_shape,
            ((HQ // 2, rows, HD), bf16),
            ((2, 4 * rows, HD), bf16),
            ((2, HD + 16, 4 * rows), bf16),
            ((rows, features), bf16),
        ],
        [
            ((KW * VOCAB, features), bf16),
            ((features, part_width), bf16),
            ((4, 8, rows), jnp.int32),
            ((2, rows, features), bf16),
            ((2, HQ // 2, rows, HD), bf16),
        ],
    )(where, ids_all, *t_pieces, *w_pieces, norm_gain[None], rope)

    att_mate, out_near = lax.optimization_barrier((att_mate, out_near))
    att_back = along(att_mate, beside)
    (att_own,) = call(
        own_kernel, "own_block", 12, 3 * 10**9, [SMEM, VMEM, VMEM, VMEM], [att_shape]
    )(where, query, keys, values)
    hidden, loss = call(
        out_kernel, "project_out", 12, 10**9,
        [SMEM, VMEM, VMEM] + piece_specs + [VMEM, VMEM, VMEM],
        [((rows, features), bf16), ((1, rows), f32)],
        [((rows, features), bf16), ((features, features), bf16)],
    )(where, att_own, att_back, *to_mate(out_own, out_near), latent, teacher[0], align)
    return hidden[None], loss


def solution(mesh):
    in_specs = (
        P("fsdp", "ctx"),
        P(),
        P("fsdp", None),
        P("fsdp", None),
        P("fsdp", None),
        P(),
        P("fsdp", "ctx", None),
        P("fsdp", "ctx"),
    )
    out_specs = (P("fsdp", "ctx", None), P("fsdp", "ctx"))
    sizes = (mesh.shape["fsdp"], mesh.shape["ctx"])
    body = functools.partial(head_body, sizes) if sizes == (2 * KW, HK) else general_body
    return jax.shard_map(body, mesh=mesh, in_specs=in_specs, out_specs=out_specs, check_vma=False)
```

```python
import functools
import math

import jax
import jax.numpy as jnp
import numpy as np
from jax import lax
from jax.experimental import pallas as pl
from jax.experimental.pallas import tpu as pltpu
from jax.sharding import PartitionSpec as P

KW = 4
HQ = 16
HK = 4
HD = 64
GROUP = HQ // HK
VOCAB = 256

theta_base = 500000.0
norm_eps = 1e-05
masked_score = -1e30
score_scale = 1.0 / math.sqrt(HD)


def rotate(values, positions):
    half_dim = values.shape[-1] // 2
    frequency = theta_base ** (-jnp.arange(half_dim, dtype=jnp.float32) * 2.0 / values.shape[-1])
    angles = positions.astype(jnp.float32)[:, None] * frequency[None, :]
    angles = jnp.concatenate([angles, angles], axis=-1)[:, None, :]
    turned = jnp.concatenate([-values[..., half_dim:], values[..., :half_dim]], axis=-1)
    return values * jnp.cos(angles) + turned * jnp.sin(angles)


def project(inputs, weight):
    return jnp.dot(
        inputs,
        lax.all_gather(weight, "fsdp", axis=0, tiled=True),
        preferred_element_type=jnp.float32,
    )


def general_body(byte_ids, byte_table, w_conv, w_qkv, w_out, norm_gain, teacher, align):
    seq_bytes = byte_ids.shape[1]
    lat_rows = seq_bytes // KW
    query_width = HQ * HD
    key_width = HK * HD
    one_hot = (
        byte_ids[0][:, None] == jnp.arange(byte_table.shape[0], dtype=jnp.int32)[None, :]
    ).astype(jnp.bfloat16)
    embedded = jnp.dot(one_hot, byte_table, preferred_element_type=jnp.float32).astype(jnp.bfloat16)
    stacked = embedded.reshape(lat_rows, KW * byte_table.shape[1])
    latent = project(stacked, w_conv).astype(jnp.bfloat16)
    latent_wide = latent.astype(jnp.float32)
    scale_rows = lax.rsqrt(jnp.mean(latent_wide * latent_wide, axis=1, keepdims=True) + norm_eps)
    normed = (latent_wide * scale_rows * norm_gain.astype(jnp.float32)[None, :]).astype(
        jnp.bfloat16
    )
    projected = project(normed, w_qkv)
    ctx_index = lax.axis_index("ctx")
    positions = ctx_index * lat_rows + jnp.arange(lat_rows, dtype=jnp.int32)
    queries = rotate(projected[:, :query_width].reshape(lat_rows, HQ, HD), positions).astype(
        jnp.bfloat16
    )
    key_rows = rotate(
        projected[:, query_width : query_width + key_width].reshape(lat_rows, HK, HD), positions
    )
    key_rows = key_rows.astype(jnp.bfloat16).reshape(lat_rows, key_width)
    value_rows = projected[:, query_width + key_width :].astype(jnp.bfloat16)
    grouped = queries.reshape(lat_rows, HK, HQ // HK, HD)
    start_state = (
        jnp.full((HK, HQ // HK, lat_rows), masked_score, jnp.float32),
        jnp.zeros((HK, HQ // HK, lat_rows), jnp.float32),
        jnp.zeros((HK, HQ // HK, lat_rows, HD), jnp.float32),
    )
    key_all = lax.all_gather(key_rows, "ctx", axis=0, tiled=True)
    value_all = lax.all_gather(value_rows, "ctx", axis=0, tiled=True)
    blocks = key_all.shape[0] // lat_rows
    key_blocks = key_all.reshape(blocks, lat_rows, HK, HD)
    value_blocks = value_all.reshape(blocks, lat_rows, HK, HD)
    block_starts = lat_rows * jnp.arange(blocks, dtype=jnp.int32)

    def one_block(partial_value, block_data):
        key_block, value_block, key_start = block_data
        row_top, row_mass, weighted = partial_value
        scores = (
            jnp.einsum("qkgd,skd->kgqs", grouped, key_block, preferred_element_type=jnp.float32)
            * score_scale
        )
        key_pos = key_start + jnp.arange(lat_rows, dtype=jnp.int32)
        allowed = key_pos[None, :] <= positions[:, None]
        scores = jnp.where(allowed[None, None], scores, masked_score)
        new_top = jnp.maximum(row_top, jnp.max(scores, axis=-1))
        weights = jnp.exp(scores - new_top[..., None])
        shrink = jnp.exp(row_top - new_top)
        row_mass = row_mass * shrink + jnp.sum(weights, axis=-1)
        weighted = weighted * shrink[..., None] + jnp.einsum(
            "kgqs,skd->kgqd",
            weights.astype(jnp.bfloat16),
            value_block,
            preferred_element_type=jnp.float32,
        )
        return ((new_top, row_mass, weighted), None)

    result, unused = lax.scan(one_block, start_state, (key_blocks, value_blocks, block_starts))
    final_top, final_mass, final_sum = result
    attended = final_sum / final_mass[..., None]
    attended = jnp.transpose(attended, (2, 0, 1, 3)).reshape(lat_rows, HQ * HD).astype(jnp.bfloat16)
    branch = project(attended, w_out)
    hidden_out = (latent_wide + branch).astype(jnp.bfloat16)
    local_rows = align[0] - ctx_index * lat_rows
    picked = jnp.take(hidden_out, local_rows, axis=0)
    difference = picked.astype(jnp.float32) - teacher[0].astype(jnp.float32)
    token_loss = jnp.mean(difference * difference, axis=1)
    return (hidden_out[None], token_loss[None])


def rope_tables(blocks, rows):
    half = HD // 2
    frequency = np.float32(theta_base) ** (-np.arange(half, dtype=np.float32) * np.float32(2.0 / HD))
    places = [np.arange(rows), np.arange(blocks) * rows]
    angles = [np.concatenate([p[:, None] * frequency[None, :].astype(np.float64)] * 4, axis=1) for p in places]
    parts = [f(angles[0]) for f in (np.cos, np.sin)] + [f(angles[1]) for f in (np.cos, np.sin)]
    return np.concatenate(parts, axis=0).astype(np.float32)


def rope_at(rope_ref, rows, block):
    blocks = (rope_ref.shape[0] - 2 * rows) // 2
    cos, sin = rope_ref[:rows, :], rope_ref[rows : 2 * rows, :]
    cos_start = rope_ref[pl.ds(2 * rows + block, 1), :]
    sin_start = rope_ref[pl.ds(2 * rows + blocks + block, 1), :]
    lane = lax.broadcasted_iota(jnp.int32, (1, 128), 1)
    sign = jnp.where((lane & (HD // 2)) == 0, -1.0, 1.0)
    return (
        cos * cos_start - sin * sin_start,
        sin * (cos_start * sign) + cos * (sin_start * sign),
    )


def turn(x, cos, sin):
    half = HD // 2
    lane = lax.broadcasted_iota(jnp.int32, x.shape, 1)
    low = (lane & half) == 0
    swapped = jnp.where(low, pltpu.roll(x, 128 - half, axis=1), pltpu.roll(x, half, axis=1))
    return x * cos + swapped * sin


def part_kernel(where_ref, qkv_ref, part_ref):
    side = where_ref[2] % 2
    start = 0
    for width in (HQ * HD, HK * HD, HK * HD):
        own = width // 2
        part_ref[:, start // 2 : start // 2 + own] = qkv_ref[
            :, pl.ds(pl.multiple_of(start + side * own, own), own)
        ]
        start += width


def table_kernel(where_ref, bytes_ref, conv_ref, total_ref, align_ref, rope_ref, out_ref, align_out, rope_out):
    align_out[...] = align_ref[...]
    rope_out[...] = rope_ref[...]
    core = where_ref[1]
    taps_in = conv_ref.shape[0]
    half = total_ref.shape[0]
    rows = pl.ds(pl.multiple_of(core * half, half), half)
    mates = bytes_ref[rows, pl.ds(pl.multiple_of((1 - core) * taps_in, taps_in), taps_in)]
    total = total_ref[...] + jnp.dot(mates, conv_ref[...], preferred_element_type=jnp.float32)
    out_ref[...] = total.astype(jnp.bfloat16)


def ordered(chip, core, pieces):
    own, near, mate_own, mate_near = pieces
    depth = own.shape[0]
    for j, (mine, mates) in enumerate(zip((own,) + near, (mate_own,) + mate_near)):
        base = (chip ^ j) * 2
        for which, piece in ((core, mine), (1 - core, mates)):
            yield pl.ds(pl.multiple_of((base + which) * depth, depth), depth), piece


def attend(queries, slots, allowed, k_s, v_s, att_ref):
    heads = HQ // 2
    rows = att_ref.shape[0]
    keys = slice(slots[0] * rows, (slots[-1] + 1) * rows)

    def score(h):
        scores = lax.dot_general(
            k_s[h // GROUP, keys, :], queries(h), (((1,), (1,)), ((), ())), preferred_element_type=jnp.float32
        )
        last = jnp.where(allowed, scores[-rows:], masked_score)
        return last if len(slots) == 1 else jnp.concatenate([scores[:-rows], last], axis=0)

    coming, results = score(0), []
    for h in range(heads):
        scores = coming
        if h + 1 < heads:
            coming = score(h + 1)
        probs = jnp.exp(scores - jnp.max(scores, axis=0, keepdims=True)).astype(jnp.bfloat16)
        total = jnp.dot(v_s[h // GROUP, :, keys], probs, preferred_element_type=jnp.float32)
        results.append(total[:HD] / total[HD : HD + 1])
        if h % 2 == 1:
            pair = jnp.transpose(jnp.concatenate(results[-2:], axis=0))
            att_ref[:, (h - 1) * HD : (h + 1) * HD] = pair.astype(jnp.bfloat16)


def causal(rows):
    return lax.broadcasted_iota(jnp.int32, (rows, rows), 0) <= lax.broadcasted_iota(
        jnp.int32, (rows, rows), 1
    )


def key_variants(ctx, which):
    for block in range(2):
        now = tuple(range(2, 3 + block))
        yield (which == block) & (ctx < 2), block, now
        yield (which == block) & (ctx >= 2), block, (0, 1) + now


def lift_kernel(
    where_ref, ids_ref, own_t, near_t, mate_own_t, mate_near_t, own_w, near_w, mate_own_w, mate_near_w,
    gain_ref, rope_ref, att_ref, query_ref, k_s, v_s, lat_ref,
    table_s, weight_s, lat_s, q_s,
):
    chip, core, ctx = where_ref[0], where_ref[1], where_ref[2]
    side, upper = ctx % 2, ctx // 2
    rows, features = lat_ref.shape
    q_width, k_width = HQ * HD // 2, HK * HD // 2
    for span, piece in ordered(chip, core, (own_t, near_t, mate_own_t, mate_near_t)):
        table_s[span, :] = piece[...]
    for span, piece in ordered(chip, core, (own_w, near_w, mate_own_w, mate_near_w)):
        weight_s[span, :] = piece[...]
    gain = gain_ref[...].astype(jnp.float32)
    v_s[:, HD:, :] = jnp.ones((v_s.shape[0], v_s.shape[1] - HD, v_s.shape[2]), jnp.bfloat16)

    def lift(slot):
        block = slot if slot < 2 else 2 * upper + slot - 2
        ids = jnp.transpose(ids_ref[block])
        byte = lax.broadcasted_iota(jnp.int32, (rows, VOCAB), 1)
        one_hot = jnp.concatenate(
            [(ids[:, k : k + 1] == byte).astype(jnp.float32).astype(jnp.bfloat16) for k in range(KW)], axis=1
        )
        latent = jnp.dot(one_hot, table_s[...], preferred_element_type=jnp.float32).astype(jnp.bfloat16)
        wide = latent.astype(jnp.float32)
        scale = lax.rsqrt(jnp.mean(wide * wide, axis=1, keepdims=True) + norm_eps)
        normed = (wide * scale * gain).astype(jnp.bfloat16)
        cos, sin = rope_at(rope_ref, rows, block)
        if slot >= 2:
            lat_s[slot - 2] = latent
            asked = jnp.dot(normed, weight_s[:, :q_width], preferred_element_type=jnp.float32)
            for pair in range(q_width // 128):
                turned = turn(asked[:, pair * 128 : (pair + 1) * 128], cos, sin)
                turned = (turned * score_scale).astype(jnp.bfloat16)
                q_s[slot - 2, 2 * pair] = turned[:, :HD]
                q_s[slot - 2, 2 * pair + 1] = turned[:, HD:]
        kept = jnp.dot(normed, weight_s[:, q_width:], preferred_element_type=jnp.float32)
        keys = turn(kept[:, :k_width], cos, sin).astype(jnp.bfloat16)
        values = jnp.transpose(kept[:, k_width:]).astype(jnp.bfloat16)
        for group in range(2):
            k_s[group, slot * rows : (slot + 1) * rows, :] = keys[:, group * HD : (group + 1) * HD]
            v_s[group, :HD, slot * rows : (slot + 1) * rows] = values[group * HD : (group + 1) * HD]

    @pl.when(upper == 1)
    def _():
        lift(0)
        lift(1)

    lift(2)
    lift(3)
    lat_ref[...] = lat_s[side]
    query_ref[...] = q_s[side]
    allowed = causal(rows)
    other = 1 - side
    for condition, block, slots in key_variants(ctx, other):

        @pl.when(condition)
        def _(block=block, slots=slots):
            attend(lambda h: q_s[block, h], slots, allowed, k_s, v_s, att_ref)


def own_kernel(where_ref, query_ref, k_ref, v_ref, att_ref):
    ctx = where_ref[2]
    allowed = causal(att_ref.shape[0])
    for condition, block, slots in key_variants(ctx, ctx % 2):

        @pl.when(condition)
        def _(slots=slots):
            attend(lambda h: query_ref[h], slots, allowed, k_ref, v_ref, att_ref)


def out_kernel(
    where_ref, own_att, mate_att, own, near, mate_own, mate_near, lat_ref, teacher_ref, align_ref,
    hidden_ref, loss_ref, att_s, weight_s,
):
    chip, core, ctx = where_ref[0], where_ref[1], where_ref[2]
    side = ctx % 2
    rows, width = lat_ref.shape
    part = own_att.shape[1]
    for span, piece in ordered(chip, core, (own, near, mate_own, mate_near)):
        weight_s[span, :] = piece[...]
    att_s[:, pl.ds(pl.multiple_of(side * part, part), part)] = own_att[...]
    att_s[:, pl.ds(pl.multiple_of((1 - side) * part, part), part)] = mate_att[...]
    branch = jnp.dot(att_s[...], weight_s[...], preferred_element_type=jnp.float32)
    hidden = (lat_ref[...].astype(jnp.float32) + branch).astype(jnp.bfloat16)
    hidden_ref[...] = hidden
    source = lax.broadcasted_iota(jnp.int32, (rows, rows), 0) + ctx * rows
    chosen = (source == align_ref[...]).astype(jnp.float32).astype(jnp.bfloat16)
    picked = lax.dot_general(
        chosen, hidden, (((0,), (0,)), ((), ())), preferred_element_type=jnp.float32
    )
    difference = picked - teacher_ref[...].astype(jnp.float32)
    square = difference * difference
    lanes = square[:, :128]
    for start in range(128, width, 128):
        lanes = lanes + square[:, start : start + 128]
    loss_ref[...] = jnp.sum(jnp.transpose(lanes), axis=0, keepdims=True) * (1.0 / width)


VMEM = pl.BlockSpec(memory_space=pltpu.VMEM)
SMEM = pl.BlockSpec(memory_space=pltpu.SMEM)
MIB = 1024 * 1024


def call(kernel, name, mib, flops, in_specs, outs, scratch=()):
    return pl.pallas_call(
        kernel,
        out_shape=tuple(jax.ShapeDtypeStruct(shape, dtype) for shape, dtype in outs),
        in_specs=in_specs,
        out_specs=(VMEM,) * len(outs),
        scratch_shapes=[pltpu.VMEM(shape, dtype) for shape, dtype in scratch],
        compiler_params=pltpu.CompilerParams(vmem_limit_bytes=mib * MIB),
        cost_estimate=pl.CostEstimate(flops=flops, bytes_accessed=4 * MIB, transcendentals=0),
        name=name,
    )


def head_body(sizes, byte_ids, byte_table, w_conv, w_qkv, w_out, norm_gain, teacher, align):
    n_fsdp, n_ctx = sizes
    me, ctx = lax.axis_index("fsdp"), lax.axis_index("ctx")
    chip, core = me // 2, me % 2
    rows = byte_ids.shape[1] // KW
    features = w_conv.shape[1]
    q_width = HQ * HD // 2
    part_width = w_qkv.shape[1] // 2
    half = VOCAB // 2
    bf16, f32 = jnp.bfloat16, jnp.float32
    where = jnp.stack([chip, core, ctx]).astype(jnp.int32)

    def swap(x, j):
        return lax.ppermute(x, "fsdp", [(d, d ^ j) for d in range(n_fsdp)])

    def along(x, pairs):
        return lax.ppermute(x, "ctx", pairs)

    def to_near(x):
        return tuple(swap(x, 2 * j) for j in range(1, n_fsdp // 2))

    def to_mate(x, near):
        return x, near, swap(x, 1), tuple(swap(piece, 1) for piece in near)

    beside = [(z, z ^ 1) for z in range(n_ctx)]

    mate_conv = swap(w_conv, 1)
    (part,) = call(
        part_kernel, "qkv_part", 4, 10**8, [SMEM, VMEM], [((w_qkv.shape[0], part_width), bf16)]
    )(where, w_qkv)
    near_w = to_near(part)

    taps_in = w_conv.shape[0]
    mine = lax.dynamic_slice(byte_table, (core * half, core * taps_in), (half, taps_in))
    total = jnp.dot(mine, w_conv, preferred_element_type=f32)
    rope = jnp.asarray(rope_tables(n_ctx, rows))
    own_t, align, rope = call(
        table_kernel, "tap_table", 8, 10**8, [SMEM] + [VMEM] * 5,
        [((half, features), bf16), (align.shape, jnp.int32), (rope.shape, f32)],
    )(where, byte_table, mate_conv, total, align, rope)
    ids = jnp.broadcast_to(byte_ids, (n_ctx, byte_ids.shape[1]))
    ids = lax.all_to_all(ids, "ctx", 0, 0, tiled=True)
    own_t, near_w, ids = lax.optimization_barrier((own_t, near_w, ids))
    near_t = to_near(own_t)
    ids = jnp.swapaxes(ids.reshape(n_ctx, rows, KW), 1, 2)
    ids = jnp.pad(ids, ((0, 0), (0, 8 - KW), (0, 0)))
    last, ids = lax.optimization_barrier((near_t[-1], ids))
    near_t = near_t[:-1] + (last,)
    t_pieces, w_pieces = to_mate(own_t, near_t), to_mate(part, near_w)
    out_own, unused = lax.optimization_barrier((w_out, near_t))
    out_near = to_near(out_own)

    near_specs = (VMEM,) * (n_fsdp // 2 - 1)
    piece_specs = [VMEM, near_specs, VMEM, near_specs]
    att_shape = ((rows, q_width), bf16)
    att_mate, query, keys, values, latent = call(
        lift_kernel, "lift", 18, 5 * 10**9,
        [SMEM, VMEM] + piece_specs + piece_specs + [VMEM, VMEM],
        [
            att_shape,
            ((HQ // 2, rows, HD), bf16),
            ((2, 4 * rows, HD), bf16),
            ((2, HD + 16, 4 * rows), bf16),
            ((rows, features), bf16),
        ],
        [
            ((KW * VOCAB, features), bf16),
            ((features, part_width), bf16),
            ((2, rows, features), bf16),
            ((2, HQ // 2, rows, HD), bf16),
        ],
    )(where, ids, *t_pieces, *w_pieces, norm_gain[None], rope)

    att_mate, out_near = lax.optimization_barrier((att_mate, out_near))
    att_back = along(att_mate, beside)
    (att_own,) = call(
        own_kernel, "own_block", 12, 3 * 10**9, [SMEM, VMEM, VMEM, VMEM], [att_shape]
    )(where, query, keys, values)
    hidden, loss = call(
        out_kernel, "project_out", 12, 10**9,
        [SMEM, VMEM, VMEM] + piece_specs + [VMEM, VMEM, VMEM],
        [((rows, features), bf16), ((1, rows), f32)],
        [((rows, features), bf16), ((features, features), bf16)],
    )(where, att_own, att_back, *to_mate(out_own, out_near), latent, teacher[0], align)
    return hidden[None], loss


def solution(mesh):
    in_specs = (
        P("fsdp", "ctx"),
        P(),
        P("fsdp", None),
        P("fsdp", None),
        P("fsdp", None),
        P(),
        P("fsdp", "ctx", None),
        P("fsdp", "ctx"),
    )
    out_specs = (P("fsdp", "ctx", None), P("fsdp", "ctx"))
    sizes = (mesh.shape["fsdp"], mesh.shape["ctx"])
    body = functools.partial(head_body, sizes) if sizes == (2 * KW, HK) else general_body
    return jax.shard_map(body, mesh=mesh, in_specs=in_specs, out_specs=out_specs, check_vma=False)
```

```python
import functools
import math

import jax
import jax.numpy as jnp
import numpy as np
from jax import lax
from jax.experimental import pallas as pl
from jax.experimental.pallas import tpu as pltpu
from jax.sharding import PartitionSpec as P

KW = 4
HQ = 16
HK = 4
HD = 64
GROUP = HQ // HK
VOCAB = 256

theta_base = 500000.0
norm_eps = 1e-05
masked_score = -1e30
score_scale = 1.0 / math.sqrt(HD)


def rotate(values, positions):
    half_dim = values.shape[-1] // 2
    frequency = theta_base ** (-jnp.arange(half_dim, dtype=jnp.float32) * 2.0 / values.shape[-1])
    angles = positions.astype(jnp.float32)[:, None] * frequency[None, :]
    angles = jnp.concatenate([angles, angles], axis=-1)[:, None, :]
    turned = jnp.concatenate([-values[..., half_dim:], values[..., :half_dim]], axis=-1)
    return values * jnp.cos(angles) + turned * jnp.sin(angles)


def project(inputs, weight):
    return jnp.dot(
        inputs,
        lax.all_gather(weight, "fsdp", axis=0, tiled=True),
        preferred_element_type=jnp.float32,
    )


def general_body(byte_ids, byte_table, w_conv, w_qkv, w_out, norm_gain, teacher, align):
    seq_bytes = byte_ids.shape[1]
    lat_rows = seq_bytes // KW
    query_width = HQ * HD
    key_width = HK * HD
    one_hot = (
        byte_ids[0][:, None] == jnp.arange(byte_table.shape[0], dtype=jnp.int32)[None, :]
    ).astype(jnp.bfloat16)
    embedded = jnp.dot(one_hot, byte_table, preferred_element_type=jnp.float32).astype(jnp.bfloat16)
    stacked = embedded.reshape(lat_rows, KW * byte_table.shape[1])
    latent = project(stacked, w_conv).astype(jnp.bfloat16)
    latent_wide = latent.astype(jnp.float32)
    scale_rows = lax.rsqrt(jnp.mean(latent_wide * latent_wide, axis=1, keepdims=True) + norm_eps)
    normed = (latent_wide * scale_rows * norm_gain.astype(jnp.float32)[None, :]).astype(
        jnp.bfloat16
    )
    projected = project(normed, w_qkv)
    ctx_index = lax.axis_index("ctx")
    positions = ctx_index * lat_rows + jnp.arange(lat_rows, dtype=jnp.int32)
    queries = rotate(projected[:, :query_width].reshape(lat_rows, HQ, HD), positions).astype(
        jnp.bfloat16
    )
    key_rows = rotate(
        projected[:, query_width : query_width + key_width].reshape(lat_rows, HK, HD), positions
    )
    key_rows = key_rows.astype(jnp.bfloat16).reshape(lat_rows, key_width)
    value_rows = projected[:, query_width + key_width :].astype(jnp.bfloat16)
    grouped = queries.reshape(lat_rows, HK, HQ // HK, HD)
    start_state = (
        jnp.full((HK, HQ // HK, lat_rows), masked_score, jnp.float32),
        jnp.zeros((HK, HQ // HK, lat_rows), jnp.float32),
        jnp.zeros((HK, HQ // HK, lat_rows, HD), jnp.float32),
    )
    key_all = lax.all_gather(key_rows, "ctx", axis=0, tiled=True)
    value_all = lax.all_gather(value_rows, "ctx", axis=0, tiled=True)
    blocks = key_all.shape[0] // lat_rows
    key_blocks = key_all.reshape(blocks, lat_rows, HK, HD)
    value_blocks = value_all.reshape(blocks, lat_rows, HK, HD)
    block_starts = lat_rows * jnp.arange(blocks, dtype=jnp.int32)

    def one_block(partial_value, block_data):
        key_block, value_block, key_start = block_data
        row_top, row_mass, weighted = partial_value
        scores = (
            jnp.einsum("qkgd,skd->kgqs", grouped, key_block, preferred_element_type=jnp.float32)
            * score_scale
        )
        key_pos = key_start + jnp.arange(lat_rows, dtype=jnp.int32)
        allowed = key_pos[None, :] <= positions[:, None]
        scores = jnp.where(allowed[None, None], scores, masked_score)
        new_top = jnp.maximum(row_top, jnp.max(scores, axis=-1))
        weights = jnp.exp(scores - new_top[..., None])
        shrink = jnp.exp(row_top - new_top)
        row_mass = row_mass * shrink + jnp.sum(weights, axis=-1)
        weighted = weighted * shrink[..., None] + jnp.einsum(
            "kgqs,skd->kgqd",
            weights.astype(jnp.bfloat16),
            value_block,
            preferred_element_type=jnp.float32,
        )
        return ((new_top, row_mass, weighted), None)

    result, unused = lax.scan(one_block, start_state, (key_blocks, value_blocks, block_starts))
    final_top, final_mass, final_sum = result
    attended = final_sum / final_mass[..., None]
    attended = jnp.transpose(attended, (2, 0, 1, 3)).reshape(lat_rows, HQ * HD).astype(jnp.bfloat16)
    branch = project(attended, w_out)
    hidden_out = (latent_wide + branch).astype(jnp.bfloat16)
    local_rows = align[0] - ctx_index * lat_rows
    picked = jnp.take(hidden_out, local_rows, axis=0)
    difference = picked.astype(jnp.float32) - teacher[0].astype(jnp.float32)
    token_loss = jnp.mean(difference * difference, axis=1)
    return (hidden_out[None], token_loss[None])


def rope_tables(blocks, rows):
    half = HD // 2
    frequency = np.float32(theta_base) ** (-np.arange(half, dtype=np.float32) * np.float32(2.0 / HD))
    places = [np.arange(rows), np.arange(blocks) * rows]
    angles = [np.concatenate([p[:, None] * frequency[None, :].astype(np.float64)] * 4, axis=1) for p in places]
    parts = [f(angles[0]) for f in (np.cos, np.sin)] + [f(angles[1]) for f in (np.cos, np.sin)]
    return np.concatenate(parts, axis=0).astype(np.float32)


def rope_at(rope_ref, rows, block):
    blocks = (rope_ref.shape[0] - 2 * rows) // 2
    cos, sin = rope_ref[:rows, :], rope_ref[rows : 2 * rows, :]
    cos_start = rope_ref[pl.ds(2 * rows + block, 1), :]
    sin_start = rope_ref[pl.ds(2 * rows + blocks + block, 1), :]
    lane = lax.broadcasted_iota(jnp.int32, (1, 128), 1)
    sign = jnp.where((lane & (HD // 2)) == 0, -1.0, 1.0)
    return (
        cos * cos_start - sin * sin_start,
        sin * (cos_start * sign) + cos * (sin_start * sign),
    )


def turn(x, cos, sin):
    half = HD // 2
    lane = lax.broadcasted_iota(jnp.int32, x.shape, 1)
    low = (lane & half) == 0
    swapped = jnp.where(low, pltpu.roll(x, 128 - half, axis=1), pltpu.roll(x, half, axis=1))
    return x * cos + swapped * sin


def part_kernel(where_ref, qkv_ref, align_ref, rope_ref, part_ref, align_out, rope_out):
    align_out[...] = align_ref[...]
    rope_out[...] = rope_ref[...]
    side = where_ref[2] % 2
    start = 0
    for width in (HQ * HD, HK * HD, HK * HD):
        own = width // 2
        part_ref[:, start // 2 : start // 2 + own] = qkv_ref[
            :, pl.ds(pl.multiple_of(start + side * own, own), own)
        ]
        start += width


def table_kernel(where_ref, bytes_ref, conv_ref, total_ref, out_ref):
    core = where_ref[1]
    taps_in = conv_ref.shape[0]
    half = total_ref.shape[0]
    rows = pl.ds(pl.multiple_of(core * half, half), half)
    mates = bytes_ref[rows, pl.ds(pl.multiple_of((1 - core) * taps_in, taps_in), taps_in)]
    total = total_ref[...] + jnp.dot(mates, conv_ref[...], preferred_element_type=jnp.float32)
    out_ref[...] = total.astype(jnp.bfloat16)


def one_hot_kernel(where_ref, ids_refs, hot_ref):
    side = where_ref[2] % 2
    length = ids_refs[0].shape[1]
    rows = length // KW
    row = lax.broadcasted_iota(jnp.int32, (rows, length), 0)
    mine = lax.broadcasted_iota(jnp.int32, (rows, length), 1) // KW == row
    tap = lax.broadcasted_iota(jnp.int32, (length, 128), 0) % KW
    pick = (tap == lax.broadcasted_iota(jnp.int32, (length, 128), 1)).astype(jnp.float32).astype(jnp.bfloat16)
    byte = lax.broadcasted_iota(jnp.int32, (rows, VOCAB), 1).astype(jnp.float32)
    for ids_ref, slot in zip(ids_refs, (2 + side, 3 - side, side, 1 - side)):
        ids = ids_ref[...].astype(jnp.float32)
        apart = jnp.where(mine, ids, 0.0).astype(jnp.bfloat16)
        columns = jnp.dot(apart, pick, preferred_element_type=jnp.float32)
        for k in range(KW):
            hot_ref[slot, :, k * VOCAB : (k + 1) * VOCAB] = (
                (columns[:, k : k + 1] == byte).astype(jnp.float32).astype(jnp.bfloat16)
            )


def ordered(chip, core, pieces):
    own, near, mate_own, mate_near = pieces
    depth = own.shape[0]
    for j, (mine, mates) in enumerate(zip((own,) + near, (mate_own,) + mate_near)):
        base = (chip ^ j) * 2
        for which, piece in ((core, mine), (1 - core, mates)):
            yield pl.ds(pl.multiple_of((base + which) * depth, depth), depth), piece


def attend(queries, slots, allowed, k_s, v_s, att_ref):
    heads = HQ // 2
    rows = att_ref.shape[0]
    keys = slice(slots[0] * rows, (slots[-1] + 1) * rows)

    def score(h):
        scores = lax.dot_general(
            k_s[h // GROUP, keys, :], queries(h), (((1,), (1,)), ((), ())), preferred_element_type=jnp.float32
        )
        last = jnp.where(allowed, scores[-rows:], masked_score)
        return last if len(slots) == 1 else jnp.concatenate([scores[:-rows], last], axis=0)

    coming, results = score(0), []
    for h in range(heads):
        scores = coming
        if h + 1 < heads:
            coming = score(h + 1)
        probs = jnp.exp(scores - jnp.max(scores, axis=0, keepdims=True)).astype(jnp.bfloat16)
        total = jnp.dot(v_s[h // GROUP, :, keys], probs, preferred_element_type=jnp.float32)
        results.append(total[:HD] / total[HD : HD + 1])
        if h % 2 == 1:
            pair = jnp.transpose(jnp.concatenate(results[-2:], axis=0))
            att_ref[:, (h - 1) * HD : (h + 1) * HD] = pair.astype(jnp.bfloat16)


def causal(rows):
    return lax.broadcasted_iota(jnp.int32, (rows, rows), 0) <= lax.broadcasted_iota(
        jnp.int32, (rows, rows), 1
    )


def key_variants(ctx, which):
    for block in range(2):
        now = tuple(range(2, 3 + block))
        yield (which == block) & (ctx < 2), block, now
        yield (which == block) & (ctx >= 2), block, (0, 1) + now


def latent_kernel(
    where_ref, hot_ref, own, near, mate_own, mate_near, gain_ref, normed_ref, lat_ref, table_s, lat_s,
):
    chip, core, ctx = where_ref[0], where_ref[1], where_ref[2]
    for span, piece in ordered(chip, core, (own, near, mate_own, mate_near)):
        table_s[span, :] = piece[...]
    gain = gain_ref[...].astype(jnp.float32)

    def latent_of(slot):
        latent = jnp.dot(hot_ref[slot], table_s[...], preferred_element_type=jnp.float32).astype(jnp.bfloat16)
        if slot >= 2:
            lat_s[slot - 2] = latent
        wide = latent.astype(jnp.float32)
        scale = lax.rsqrt(jnp.mean(wide * wide, axis=1, keepdims=True) + norm_eps)
        normed_ref[slot] = (wide * scale * gain).astype(jnp.bfloat16)

    @pl.when(ctx >= 2)
    def _():
        latent_of(0)
        latent_of(1)

    latent_of(2)
    latent_of(3)
    lat_ref[...] = lat_s[ctx % 2]


def lift_kernel(
    where_ref, normed_ref, own, near, mate_own, mate_near, rope_ref, att_ref, query_ref, k_s, v_s, weight_s, q_s,
):
    chip, core, ctx = where_ref[0], where_ref[1], where_ref[2]
    side, upper = ctx % 2, ctx // 2
    rows = att_ref.shape[0]
    q_width, k_width = HQ * HD // 2, HK * HD // 2
    for span, piece in ordered(chip, core, (own, near, mate_own, mate_near)):
        weight_s[span, :] = piece[...]
    v_s[:, HD:, :] = jnp.ones((v_s.shape[0], v_s.shape[1] - HD, v_s.shape[2]), jnp.bfloat16)

    def lift(slot):
        block = slot if slot < 2 else 2 * upper + slot - 2
        normed = normed_ref[slot]
        cos, sin = rope_at(rope_ref, rows, block)
        if slot >= 2:
            asked = jnp.dot(normed, weight_s[:, :q_width], preferred_element_type=jnp.float32)
            for pair in range(q_width // 128):
                turned = turn(asked[:, pair * 128 : (pair + 1) * 128], cos, sin)
                turned = (turned * score_scale).astype(jnp.bfloat16)
                q_s[slot - 2, 2 * pair] = turned[:, :HD]
                q_s[slot - 2, 2 * pair + 1] = turned[:, HD:]
        kept = jnp.dot(normed, weight_s[:, q_width:], preferred_element_type=jnp.float32)
        keys = turn(kept[:, :k_width], cos, sin).astype(jnp.bfloat16)
        values = jnp.transpose(kept[:, k_width:]).astype(jnp.bfloat16)
        for group in range(2):
            k_s[group, slot * rows : (slot + 1) * rows, :] = keys[:, group * HD : (group + 1) * HD]
            v_s[group, :HD, slot * rows : (slot + 1) * rows] = values[group * HD : (group + 1) * HD]

    @pl.when(upper == 1)
    def _():
        lift(0)
        lift(1)

    lift(2)
    lift(3)
    query_ref[...] = q_s[side]
    allowed = causal(rows)
    other = 1 - side
    for condition, block, slots in key_variants(ctx, other):

        @pl.when(condition)
        def _(block=block, slots=slots):
            attend(lambda h: q_s[block, h], slots, allowed, k_s, v_s, att_ref)


def own_kernel(where_ref, query_ref, k_ref, v_ref, att_ref):
    ctx = where_ref[2]
    allowed = causal(att_ref.shape[0])
    for condition, block, slots in key_variants(ctx, ctx % 2):

        @pl.when(condition)
        def _(slots=slots):
            attend(lambda h: query_ref[h], slots, allowed, k_ref, v_ref, att_ref)


def out_kernel(
    where_ref, own_att, mate_att, own, near, mate_own, mate_near, lat_ref, teacher_ref, align_ref,
    hidden_ref, loss_ref, att_s, weight_s,
):
    chip, core, ctx = where_ref[0], where_ref[1], where_ref[2]
    side = ctx % 2
    rows, width = lat_ref.shape
    part = own_att.shape[1]
    for span, piece in ordered(chip, core, (own, near, mate_own, mate_near)):
        weight_s[span, :] = piece[...]
    att_s[:, pl.ds(pl.multiple_of(side * part, part), part)] = own_att[...]
    att_s[:, pl.ds(pl.multiple_of((1 - side) * part, part), part)] = mate_att[...]
    branch = jnp.dot(att_s[...], weight_s[...], preferred_element_type=jnp.float32)
    hidden = (lat_ref[...].astype(jnp.float32) + branch).astype(jnp.bfloat16)
    hidden_ref[...] = hidden
    source = lax.broadcasted_iota(jnp.int32, (rows, rows), 0) + ctx * rows
    chosen = (source == align_ref[...]).astype(jnp.float32).astype(jnp.bfloat16)
    picked = lax.dot_general(
        chosen, hidden, (((0,), (0,)), ((), ())), preferred_element_type=jnp.float32
    )
    difference = picked - teacher_ref[...].astype(jnp.float32)
    square = difference * difference
    lanes = square[:, :128]
    for start in range(128, width, 128):
        lanes = lanes + square[:, start : start + 128]
    loss_ref[...] = jnp.sum(jnp.transpose(lanes), axis=0, keepdims=True) * (1.0 / width)


VMEM = pl.BlockSpec(memory_space=pltpu.VMEM)
SMEM = pl.BlockSpec(memory_space=pltpu.SMEM)
MIB = 1024 * 1024


def call(kernel, name, mib, flops, in_specs, outs, scratch=()):
    return pl.pallas_call(
        kernel,
        out_shape=tuple(jax.ShapeDtypeStruct(shape, dtype) for shape, dtype in outs),
        in_specs=in_specs,
        out_specs=(VMEM,) * len(outs),
        scratch_shapes=[pltpu.VMEM(shape, dtype) for shape, dtype in scratch],
        compiler_params=pltpu.CompilerParams(vmem_limit_bytes=mib * MIB),
        cost_estimate=pl.CostEstimate(flops=flops, bytes_accessed=4 * MIB, transcendentals=0),
        name=name,
    )


def head_body(sizes, byte_ids, byte_table, w_conv, w_qkv, w_out, norm_gain, teacher, align):
    n_fsdp, n_ctx = sizes
    me, ctx = lax.axis_index("fsdp"), lax.axis_index("ctx")
    chip, core = me // 2, me % 2
    rows = byte_ids.shape[1] // KW
    features = w_conv.shape[1]
    q_width = HQ * HD // 2
    part_width = w_qkv.shape[1] // 2
    half = VOCAB // 2
    bf16, f32 = jnp.bfloat16, jnp.float32
    where = jnp.stack([chip, core, ctx]).astype(jnp.int32)

    def swap(x, j):
        return lax.ppermute(x, "fsdp", [(d, d ^ j) for d in range(n_fsdp)])

    def along(x, pairs):
        return lax.ppermute(x, "ctx", pairs)

    def to_near(x):
        return tuple(swap(x, 2 * j) for j in range(1, n_fsdp // 2))

    def to_mate(x, near):
        return x, near, swap(x, 1), tuple(swap(piece, 1) for piece in near)

    beside = [(z, z ^ 1) for z in range(n_ctx)]

    mate_conv = swap(w_conv, 1)
    taps_in = w_conv.shape[0]
    mine = lax.dynamic_slice(byte_table, (core * half, core * taps_in), (half, taps_in))
    total = jnp.dot(mine, w_conv, preferred_element_type=f32)
    rope = jnp.asarray(rope_tables(n_ctx, rows))
    (own_t,) = call(
        table_kernel, "tap_table", 8, 10**8, [SMEM, VMEM, VMEM, VMEM], [((half, features), bf16)]
    )(where, byte_table, mate_conv, total)
    near_t = to_near(own_t)

    ids, late_qkv, unused = lax.optimization_barrier((byte_ids, w_qkv, own_t))
    ids_all = (
        ids,
        along(ids, beside),
        along(ids, [(0, 2), (1, 3)]),
        along(ids, [(0, 3), (1, 2)]),
    )
    (hot,) = call(
        one_hot_kernel, "one_hot", 8, 10**9, [SMEM, (VMEM,) * 4], [((n_ctx, rows, KW * VOCAB), bf16)]
    )(where, ids_all)
    part, align, rope = call(
        part_kernel, "qkv_part", 6, 10**8, [SMEM, VMEM, VMEM, VMEM],
        [((w_qkv.shape[0], part_width), bf16), (align.shape, jnp.int32), (rope.shape, f32)],
    )(where, late_qkv, align, rope)
    last, hot, part = lax.optimization_barrier((near_t[-1], hot, part))
    near_t = near_t[:-1] + (last,)
    part, unused = lax.optimization_barrier((part, near_t))
    near_w = to_near(part)

    near_specs = (VMEM,) * (n_fsdp // 2 - 1)
    piece_specs = [VMEM, near_specs, VMEM, near_specs]
    normed, latent = call(
        latent_kernel, "latents", 18, 2 * 10**9,
        [SMEM, VMEM] + piece_specs + [VMEM],
        [((n_ctx, rows, features), bf16), ((rows, features), bf16)],
        [((KW * VOCAB, features), bf16), ((2, rows, features), bf16)],
    )(where, hot, *to_mate(own_t, near_t), norm_gain[None])
    near_w, normed = lax.optimization_barrier((near_w, normed))
    out_own, unused = lax.optimization_barrier((w_out, near_w))
    out_near = to_near(out_own)

    att_shape = ((rows, q_width), bf16)
    att_mate, query, keys, values = call(
        lift_kernel, "lift", 16, 4 * 10**9,
        [SMEM, VMEM] + piece_specs + [VMEM],
        [
            att_shape,
            ((HQ // 2, rows, HD), bf16),
            ((2, 4 * rows, HD), bf16),
            ((2, HD + 16, 4 * rows), bf16),
        ],
        [((features, part_width), bf16), ((2, HQ // 2, rows, HD), bf16)],
    )(where, normed, *to_mate(part, near_w), rope)

    att_mate, out_near = lax.optimization_barrier((att_mate, out_near))
    att_back = along(att_mate, beside)
    (att_own,) = call(
        own_kernel, "own_block", 12, 3 * 10**9, [SMEM, VMEM, VMEM, VMEM], [att_shape]
    )(where, query, keys, values)
    hidden, loss = call(
        out_kernel, "project_out", 12, 10**9,
        [SMEM, VMEM, VMEM] + piece_specs + [VMEM, VMEM, VMEM],
        [((rows, features), bf16), ((1, rows), f32)],
        [((rows, features), bf16), ((features, features), bf16)],
    )(where, att_own, att_back, *to_mate(out_own, out_near), latent, teacher[0], align)
    return hidden[None], loss


def solution(mesh):
    in_specs = (
        P("fsdp", "ctx"),
        P(),
        P("fsdp", None),
        P("fsdp", None),
        P("fsdp", None),
        P(),
        P("fsdp", "ctx", None),
        P("fsdp", "ctx"),
    )
    out_specs = (P("fsdp", "ctx", None), P("fsdp", "ctx"))
    sizes = (mesh.shape["fsdp"], mesh.shape["ctx"])
    body = functools.partial(head_body, sizes) if sizes == (2 * KW, HK) else general_body
    return jax.shard_map(body, mesh=mesh, in_specs=in_specs, out_specs=out_specs, check_vma=False)
```

```python
import functools
import math

import jax
import jax.numpy as jnp
import numpy as np
from jax import lax
from jax.experimental import pallas as pl
from jax.experimental.pallas import tpu as pltpu
from jax.sharding import PartitionSpec as P

KW = 4
HQ = 16
HK = 4
HD = 64
GROUP = HQ // HK
VOCAB = 256

theta_base = 500000.0
norm_eps = 1e-05
masked_score = -1e30
score_scale = 1.0 / math.sqrt(HD)


def rotate(values, positions):
    half_dim = values.shape[-1] // 2
    frequency = theta_base ** (-jnp.arange(half_dim, dtype=jnp.float32) * 2.0 / values.shape[-1])
    angles = positions.astype(jnp.float32)[:, None] * frequency[None, :]
    angles = jnp.concatenate([angles, angles], axis=-1)[:, None, :]
    turned = jnp.concatenate([-values[..., half_dim:], values[..., :half_dim]], axis=-1)
    return values * jnp.cos(angles) + turned * jnp.sin(angles)


def project(inputs, weight):
    return jnp.dot(
        inputs,
        lax.all_gather(weight, "fsdp", axis=0, tiled=True),
        preferred_element_type=jnp.float32,
    )


def general_body(byte_ids, byte_table, w_conv, w_qkv, w_out, norm_gain, teacher, align):
    seq_bytes = byte_ids.shape[1]
    lat_rows = seq_bytes // KW
    query_width = HQ * HD
    key_width = HK * HD
    one_hot = (
        byte_ids[0][:, None] == jnp.arange(byte_table.shape[0], dtype=jnp.int32)[None, :]
    ).astype(jnp.bfloat16)
    embedded = jnp.dot(one_hot, byte_table, preferred_element_type=jnp.float32).astype(jnp.bfloat16)
    stacked = embedded.reshape(lat_rows, KW * byte_table.shape[1])
    latent = project(stacked, w_conv).astype(jnp.bfloat16)
    latent_wide = latent.astype(jnp.float32)
    scale_rows = lax.rsqrt(jnp.mean(latent_wide * latent_wide, axis=1, keepdims=True) + norm_eps)
    normed = (latent_wide * scale_rows * norm_gain.astype(jnp.float32)[None, :]).astype(
        jnp.bfloat16
    )
    projected = project(normed, w_qkv)
    ctx_index = lax.axis_index("ctx")
    positions = ctx_index * lat_rows + jnp.arange(lat_rows, dtype=jnp.int32)
    queries = rotate(projected[:, :query_width].reshape(lat_rows, HQ, HD), positions).astype(
        jnp.bfloat16
    )
    key_rows = rotate(
        projected[:, query_width : query_width + key_width].reshape(lat_rows, HK, HD), positions
    )
    key_rows = key_rows.astype(jnp.bfloat16).reshape(lat_rows, key_width)
    value_rows = projected[:, query_width + key_width :].astype(jnp.bfloat16)
    grouped = queries.reshape(lat_rows, HK, HQ // HK, HD)
    start_state = (
        jnp.full((HK, HQ // HK, lat_rows), masked_score, jnp.float32),
        jnp.zeros((HK, HQ // HK, lat_rows), jnp.float32),
        jnp.zeros((HK, HQ // HK, lat_rows, HD), jnp.float32),
    )
    key_all = lax.all_gather(key_rows, "ctx", axis=0, tiled=True)
    value_all = lax.all_gather(value_rows, "ctx", axis=0, tiled=True)
    blocks = key_all.shape[0] // lat_rows
    key_blocks = key_all.reshape(blocks, lat_rows, HK, HD)
    value_blocks = value_all.reshape(blocks, lat_rows, HK, HD)
    block_starts = lat_rows * jnp.arange(blocks, dtype=jnp.int32)

    def one_block(partial_value, block_data):
        key_block, value_block, key_start = block_data
        row_top, row_mass, weighted = partial_value
        scores = (
            jnp.einsum("qkgd,skd->kgqs", grouped, key_block, preferred_element_type=jnp.float32)
            * score_scale
        )
        key_pos = key_start + jnp.arange(lat_rows, dtype=jnp.int32)
        allowed = key_pos[None, :] <= positions[:, None]
        scores = jnp.where(allowed[None, None], scores, masked_score)
        new_top = jnp.maximum(row_top, jnp.max(scores, axis=-1))
        weights = jnp.exp(scores - new_top[..., None])
        shrink = jnp.exp(row_top - new_top)
        row_mass = row_mass * shrink + jnp.sum(weights, axis=-1)
        weighted = weighted * shrink[..., None] + jnp.einsum(
            "kgqs,skd->kgqd",
            weights.astype(jnp.bfloat16),
            value_block,
            preferred_element_type=jnp.float32,
        )
        return ((new_top, row_mass, weighted), None)

    result, unused = lax.scan(one_block, start_state, (key_blocks, value_blocks, block_starts))
    final_top, final_mass, final_sum = result
    attended = final_sum / final_mass[..., None]
    attended = jnp.transpose(attended, (2, 0, 1, 3)).reshape(lat_rows, HQ * HD).astype(jnp.bfloat16)
    branch = project(attended, w_out)
    hidden_out = (latent_wide + branch).astype(jnp.bfloat16)
    local_rows = align[0] - ctx_index * lat_rows
    picked = jnp.take(hidden_out, local_rows, axis=0)
    difference = picked.astype(jnp.float32) - teacher[0].astype(jnp.float32)
    token_loss = jnp.mean(difference * difference, axis=1)
    return (hidden_out[None], token_loss[None])


def rope_tables(blocks, rows):
    half = HD // 2
    frequency = np.float32(theta_base) ** (-np.arange(half, dtype=np.float32) * np.float32(2.0 / HD))
    places = [np.arange(rows), np.arange(blocks) * rows]
    angles = [np.concatenate([p[:, None] * frequency[None, :].astype(np.float64)] * 4, axis=1) for p in places]
    parts = [f(angles[0]) for f in (np.cos, np.sin)] + [f(angles[1]) for f in (np.cos, np.sin)]
    return np.concatenate(parts, axis=0).astype(np.float32)


def rope_at(rope_ref, rows, block):
    blocks = (rope_ref.shape[0] - 2 * rows) // 2
    cos, sin = rope_ref[:rows, :], rope_ref[rows : 2 * rows, :]
    cos_start = rope_ref[pl.ds(2 * rows + block, 1), :]
    sin_start = rope_ref[pl.ds(2 * rows + blocks + block, 1), :]
    lane = lax.broadcasted_iota(jnp.int32, (1, 128), 1)
    sign = jnp.where((lane & (HD // 2)) == 0, -1.0, 1.0)
    return (
        cos * cos_start - sin * sin_start,
        sin * (cos_start * sign) + cos * (sin_start * sign),
    )


def turn(x, cos, sin):
    half = HD // 2
    lane = lax.broadcasted_iota(jnp.int32, x.shape, 1)
    low = (lane & half) == 0
    swapped = jnp.where(low, pltpu.roll(x, 128 - half, axis=1), pltpu.roll(x, half, axis=1))
    return x * cos + swapped * sin


def part_kernel(where_ref, qkv_ref, align_ref, rope_ref, part_ref, align_out, rope_out):
    align_out[...] = align_ref[...]
    rope_out[...] = rope_ref[...]
    side = where_ref[2] % 2
    start = 0
    for width in (HQ * HD, HK * HD, HK * HD):
        own = width // 2
        part_ref[:, start // 2 : start // 2 + own] = qkv_ref[
            :, pl.ds(pl.multiple_of(start + side * own, own), own)
        ]
        start += width


def table_kernel(where_ref, bytes_ref, conv_ref, total_ref, out_ref):
    core = where_ref[1]
    taps_in = conv_ref.shape[0]
    half = total_ref.shape[0]
    rows = pl.ds(pl.multiple_of(core * half, half), half)
    mates = bytes_ref[rows, pl.ds(pl.multiple_of((1 - core) * taps_in, taps_in), taps_in)]
    total = total_ref[...] + jnp.dot(mates, conv_ref[...], preferred_element_type=jnp.float32)
    out_ref[...] = total.astype(jnp.bfloat16)


def one_hot_kernel(where_ref, ids_refs, hot_ref):
    side = where_ref[2] % 2
    length = ids_refs[0].shape[1]
    rows = length // KW
    row = lax.broadcasted_iota(jnp.int32, (rows, length), 0)
    mine = lax.broadcasted_iota(jnp.int32, (rows, length), 1) // KW == row
    tap = lax.broadcasted_iota(jnp.int32, (length, 128), 0) % KW
    pick = (tap == lax.broadcasted_iota(jnp.int32, (length, 128), 1)).astype(jnp.float32).astype(jnp.bfloat16)
    byte = lax.broadcasted_iota(jnp.int32, (rows, VOCAB), 1).astype(jnp.float32)
    for ids_ref, slot in zip(ids_refs, (2 + side, 3 - side, side, 1 - side)):
        ids = ids_ref[...].astype(jnp.float32)
        apart = jnp.where(mine, ids, 0.0).astype(jnp.bfloat16)
        columns = jnp.dot(apart, pick, preferred_element_type=jnp.float32)
        for k in range(KW):
            hot_ref[slot, :, k * VOCAB : (k + 1) * VOCAB] = (
                (columns[:, k : k + 1] == byte).astype(jnp.float32).astype(jnp.bfloat16)
            )


def ordered(chip, core, pieces):
    own, near, mate_own, mate_near = pieces
    depth = own.shape[0]
    for j, (mine, mates) in enumerate(zip((own,) + near, (mate_own,) + mate_near)):
        base = (chip ^ j) * 2
        for which, piece in ((core, mine), (1 - core, mates)):
            yield pl.ds(pl.multiple_of((base + which) * depth, depth), depth), piece


def attend(queries, slots, allowed, k_s, v_s, att_ref):
    heads = HQ // 2
    rows = att_ref.shape[0]
    keys = slice(slots[0] * rows, (slots[-1] + 1) * rows)

    def score(h):
        scores = lax.dot_general(
            k_s[h // GROUP, keys, :], queries(h), (((1,), (1,)), ((), ())), preferred_element_type=jnp.float32
        )
        last = jnp.where(allowed, scores[-rows:], masked_score)
        return last if len(slots) == 1 else jnp.concatenate([scores[:-rows], last], axis=0)

    coming, results = score(0), []
    for h in range(heads):
        scores = coming
        if h + 1 < heads:
            coming = score(h + 1)
        probs = jnp.exp(scores - jnp.max(scores, axis=0, keepdims=True)).astype(jnp.bfloat16)
        total = jnp.dot(v_s[h // GROUP, :, keys], probs, preferred_element_type=jnp.float32)
        results.append(total[:HD] / total[HD : HD + 1])
        if h % 2 == 1:
            pair = jnp.transpose(jnp.concatenate(results[-2:], axis=0))
            att_ref[:, (h - 1) * HD : (h + 1) * HD] = pair.astype(jnp.bfloat16)


def causal(rows):
    return lax.broadcasted_iota(jnp.int32, (rows, rows), 0) <= lax.broadcasted_iota(
        jnp.int32, (rows, rows), 1
    )


def key_variants(ctx, which):
    for block in range(2):
        now = tuple(range(2, 3 + block))
        yield (which == block) & (ctx < 2), block, now
        yield (which == block) & (ctx >= 2), block, (0, 1) + now


def latent_kernel(
    where_ref, hot_ref, own, near, mate_own, mate_near, gain_ref, normed_ref, lat_ref, table_s, lat_s,
):
    chip, core, ctx = where_ref[0], where_ref[1], where_ref[2]
    for span, piece in ordered(chip, core, (own, near, mate_own, mate_near)):
        table_s[span, :] = piece[...]
    gain = gain_ref[...].astype(jnp.float32)

    def latent_of(slot):
        latent = jnp.dot(hot_ref[slot], table_s[...], preferred_element_type=jnp.float32).astype(jnp.bfloat16)
        if slot >= 2:
            lat_s[slot - 2] = latent
        wide = latent.astype(jnp.float32)
        scale = lax.rsqrt(jnp.mean(wide * wide, axis=1, keepdims=True) + norm_eps)
        normed_ref[slot] = (wide * scale * gain).astype(jnp.bfloat16)

    @pl.when(ctx >= 2)
    def _():
        latent_of(0)
        latent_of(1)

    latent_of(2)
    latent_of(3)
    lat_ref[...] = lat_s[ctx % 2]


def lift_kernel(
    where_ref, normed_ref, own, near, mate_own, mate_near, rope_ref, att_ref, query_ref, k_s, v_s, weight_s, q_s,
):
    chip, core, ctx = where_ref[0], where_ref[1], where_ref[2]
    side, upper = ctx % 2, ctx // 2
    rows = att_ref.shape[0]
    q_width, k_width = HQ * HD // 2, HK * HD // 2
    for span, piece in ordered(chip, core, (own, near, mate_own, mate_near)):
        weight_s[span, :] = piece[...]
    v_s[:, HD:, :] = jnp.ones((v_s.shape[0], v_s.shape[1] - HD, v_s.shape[2]), jnp.bfloat16)

    def lift(slot):
        block = slot if slot < 2 else 2 * upper + slot - 2
        normed = normed_ref[slot]
        cos, sin = rope_at(rope_ref, rows, block)
        if slot >= 2:
            asked = jnp.dot(normed, weight_s[:, :q_width], preferred_element_type=jnp.float32)
            for pair in range(q_width // 128):
                turned = turn(asked[:, pair * 128 : (pair + 1) * 128], cos, sin)
                turned = (turned * score_scale).astype(jnp.bfloat16)
                q_s[slot - 2, 2 * pair] = turned[:, :HD]
                q_s[slot - 2, 2 * pair + 1] = turned[:, HD:]
        kept = jnp.dot(normed, weight_s[:, q_width:], preferred_element_type=jnp.float32)
        keys = turn(kept[:, :k_width], cos, sin).astype(jnp.bfloat16)
        values = jnp.transpose(kept[:, k_width:]).astype(jnp.bfloat16)
        for group in range(2):
            k_s[group, slot * rows : (slot + 1) * rows, :] = keys[:, group * HD : (group + 1) * HD]
            v_s[group, :HD, slot * rows : (slot + 1) * rows] = values[group * HD : (group + 1) * HD]

    @pl.when(upper == 1)
    def _():
        lift(0)
        lift(1)

    lift(2)
    lift(3)
    query_ref[...] = q_s[side]
    allowed = causal(rows)
    other = 1 - side
    for condition, block, slots in key_variants(ctx, other):

        @pl.when(condition)
        def _(block=block, slots=slots):
            attend(lambda h: q_s[block, h], slots, allowed, k_s, v_s, att_ref)


def own_kernel(where_ref, query_ref, k_ref, v_ref, att_ref):
    ctx = where_ref[2]
    allowed = causal(att_ref.shape[0])
    for condition, block, slots in key_variants(ctx, ctx % 2):

        @pl.when(condition)
        def _(slots=slots):
            attend(lambda h: query_ref[h], slots, allowed, k_ref, v_ref, att_ref)


def out_kernel(
    where_ref, own_att, mate_att, own, near, mate_own, mate_near, lat_ref, teacher_ref, align_ref,
    hidden_ref, loss_ref, att_s, weight_s,
):
    chip, core, ctx = where_ref[0], where_ref[1], where_ref[2]
    side = ctx % 2
    rows, width = lat_ref.shape
    part = own_att.shape[1]
    for span, piece in ordered(chip, core, (own, near, mate_own, mate_near)):
        weight_s[span, :] = piece[...]
    att_s[:, pl.ds(pl.multiple_of(side * part, part), part)] = own_att[...]
    att_s[:, pl.ds(pl.multiple_of((1 - side) * part, part), part)] = mate_att[...]
    branch = jnp.dot(att_s[...], weight_s[...], preferred_element_type=jnp.float32)
    hidden = (lat_ref[...].astype(jnp.float32) + branch).astype(jnp.bfloat16)
    hidden_ref[...] = hidden
    source = lax.broadcasted_iota(jnp.int32, (rows, rows), 0) + ctx * rows
    chosen = (source == align_ref[...]).astype(jnp.float32).astype(jnp.bfloat16)
    picked = lax.dot_general(
        chosen, hidden, (((0,), (0,)), ((), ())), preferred_element_type=jnp.float32
    )
    difference = picked - teacher_ref[...].astype(jnp.float32)
    square = difference * difference
    lanes = square[:, :128]
    for start in range(128, width, 128):
        lanes = lanes + square[:, start : start + 128]
    loss_ref[...] = jnp.sum(jnp.transpose(lanes), axis=0, keepdims=True) * (1.0 / width)


VMEM = pl.BlockSpec(memory_space=pltpu.VMEM)
SMEM = pl.BlockSpec(memory_space=pltpu.SMEM)
MIB = 1024 * 1024


def call(kernel, name, mib, flops, in_specs, outs, scratch=()):
    return pl.pallas_call(
        kernel,
        out_shape=tuple(jax.ShapeDtypeStruct(shape, dtype) for shape, dtype in outs),
        in_specs=in_specs,
        out_specs=(VMEM,) * len(outs),
        scratch_shapes=[pltpu.VMEM(shape, dtype) for shape, dtype in scratch],
        compiler_params=pltpu.CompilerParams(vmem_limit_bytes=mib * MIB),
        cost_estimate=pl.CostEstimate(flops=flops, bytes_accessed=4 * MIB, transcendentals=0),
        name=name,
    )


def head_body(sizes, byte_ids, byte_table, w_conv, w_qkv, w_out, norm_gain, teacher, align):
    n_fsdp, n_ctx = sizes
    me, ctx = lax.axis_index("fsdp"), lax.axis_index("ctx")
    chip, core = me // 2, me % 2
    rows = byte_ids.shape[1] // KW
    features = w_conv.shape[1]
    q_width = HQ * HD // 2
    part_width = w_qkv.shape[1] // 2
    half = VOCAB // 2
    bf16, f32 = jnp.bfloat16, jnp.float32
    where = jnp.stack([chip, core, ctx]).astype(jnp.int32)

    def swap(x, j):
        return lax.ppermute(x, "fsdp", [(d, d ^ j) for d in range(n_fsdp)])

    def along(x, pairs):
        return lax.ppermute(x, "ctx", pairs)

    def to_near(x):
        return tuple(swap(x, 2 * j) for j in range(1, n_fsdp // 2))

    def to_mate(x, near):
        return x, near, swap(x, 1), tuple(swap(piece, 1) for piece in near)

    beside = [(z, z ^ 1) for z in range(n_ctx)]

    mate_conv = swap(w_conv, 1)
    taps_in = w_conv.shape[0]
    mine = lax.dynamic_slice(byte_table, (core * half, core * taps_in), (half, taps_in))
    total = jnp.dot(mine, w_conv, preferred_element_type=f32)
    rope = jnp.asarray(rope_tables(n_ctx, rows))
    (own_t,) = call(
        table_kernel, "tap_table", 8, 10**8, [SMEM, VMEM, VMEM, VMEM], [((half, features), bf16)]
    )(where, byte_table, mate_conv, total)
    near_t = to_near(own_t)

    ids, late_qkv, unused = lax.optimization_barrier((byte_ids, w_qkv, own_t))
    ids_all = (
        ids,
        along(ids, beside),
        along(ids, [(0, 2), (1, 3)]),
        along(ids, [(0, 3), (1, 2)]),
    )
    (hot,) = call(
        one_hot_kernel, "one_hot", 8, 10**9, [SMEM, (VMEM,) * 4], [((n_ctx, rows, KW * VOCAB), bf16)]
    )(where, ids_all)
    part, align, rope = call(
        part_kernel, "qkv_part", 6, 10**8, [SMEM, VMEM, VMEM, VMEM],
        [((w_qkv.shape[0], part_width), bf16), (align.shape, jnp.int32), (rope.shape, f32)],
    )(where, late_qkv, align, rope)
    last, hot, part = lax.optimization_barrier((near_t[-1], hot, part))
    near_t = near_t[:-1] + (last,)
    part, unused = lax.optimization_barrier((part, near_t))
    near_w = to_near(part)

    near_specs = (VMEM,) * (n_fsdp // 2 - 1)
    piece_specs = [VMEM, near_specs, VMEM, near_specs]
    normed, latent = call(
        latent_kernel, "latents", 18, 2 * 10**9,
        [SMEM, VMEM] + piece_specs + [VMEM],
        [((n_ctx, rows, features), bf16), ((rows, features), bf16)],
        [((KW * VOCAB, features), bf16), ((2, rows, features), bf16)],
    )(where, hot, *to_mate(own_t, near_t), norm_gain[None])
    near_w, normed = lax.optimization_barrier((near_w, normed))
    out_own, unused = lax.optimization_barrier((w_out, near_w))
    out_near = to_near(out_own)

    att_shape = ((rows, q_width), bf16)
    att_mate, query, keys, values = call(
        lift_kernel, "lift", 16, 4 * 10**9,
        [SMEM, VMEM] + piece_specs + [VMEM],
        [
            att_shape,
            ((HQ // 2, rows, HD), bf16),
            ((2, 4 * rows, HD), bf16),
            ((2, HD + 16, 4 * rows), bf16),
        ],
        [((features, part_width), bf16), ((2, HQ // 2, rows, HD), bf16)],
    )(where, normed, *to_mate(part, near_w), rope)

    att_back = along(att_mate, beside)
    (att_own,) = call(
        own_kernel, "own_block", 12, 3 * 10**9, [SMEM, VMEM, VMEM, VMEM], [att_shape]
    )(where, query, keys, values)
    att_own, out_near = lax.optimization_barrier((att_own, out_near))
    hidden, loss = call(
        out_kernel, "project_out", 12, 10**9,
        [SMEM, VMEM, VMEM] + piece_specs + [VMEM, VMEM, VMEM],
        [((rows, features), bf16), ((1, rows), f32)],
        [((rows, features), bf16), ((features, features), bf16)],
    )(where, att_own, att_back, *to_mate(out_own, out_near), latent, teacher[0], align)
    return hidden[None], loss


def solution(mesh):
    in_specs = (
        P("fsdp", "ctx"),
        P(),
        P("fsdp", None),
        P("fsdp", None),
        P("fsdp", None),
        P(),
        P("fsdp", "ctx", None),
        P("fsdp", "ctx"),
    )
    out_specs = (P("fsdp", "ctx", None), P("fsdp", "ctx"))
    sizes = (mesh.shape["fsdp"], mesh.shape["ctx"])
    body = functools.partial(head_body, sizes) if sizes == (2 * KW, HK) else general_body
    return jax.shard_map(body, mesh=mesh, in_specs=in_specs, out_specs=out_specs, check_vma=False)
```

```python
import functools
import math

import jax
import jax.numpy as jnp
import numpy as np
from jax import lax
from jax.experimental import pallas as pl
from jax.experimental.pallas import tpu as pltpu
from jax.sharding import PartitionSpec as P

KW = 4
HQ = 16
HK = 4
HD = 64
GROUP = HQ // HK
VOCAB = 256

theta_base = 500000.0
norm_eps = 1e-05
masked_score = -1e30
score_scale = 1.0 / math.sqrt(HD)


def rotate(values, positions):
    half_dim = values.shape[-1] // 2
    frequency = theta_base ** (-jnp.arange(half_dim, dtype=jnp.float32) * 2.0 / values.shape[-1])
    angles = positions.astype(jnp.float32)[:, None] * frequency[None, :]
    angles = jnp.concatenate([angles, angles], axis=-1)[:, None, :]
    turned = jnp.concatenate([-values[..., half_dim:], values[..., :half_dim]], axis=-1)
    return values * jnp.cos(angles) + turned * jnp.sin(angles)


def project(inputs, weight):
    return jnp.dot(
        inputs,
        lax.all_gather(weight, "fsdp", axis=0, tiled=True),
        preferred_element_type=jnp.float32,
    )


def general_body(byte_ids, byte_table, w_conv, w_qkv, w_out, norm_gain, teacher, align):
    seq_bytes = byte_ids.shape[1]
    lat_rows = seq_bytes // KW
    query_width = HQ * HD
    key_width = HK * HD
    one_hot = (
        byte_ids[0][:, None] == jnp.arange(byte_table.shape[0], dtype=jnp.int32)[None, :]
    ).astype(jnp.bfloat16)
    embedded = jnp.dot(one_hot, byte_table, preferred_element_type=jnp.float32).astype(jnp.bfloat16)
    stacked = embedded.reshape(lat_rows, KW * byte_table.shape[1])
    latent = project(stacked, w_conv).astype(jnp.bfloat16)
    latent_wide = latent.astype(jnp.float32)
    scale_rows = lax.rsqrt(jnp.mean(latent_wide * latent_wide, axis=1, keepdims=True) + norm_eps)
    normed = (latent_wide * scale_rows * norm_gain.astype(jnp.float32)[None, :]).astype(
        jnp.bfloat16
    )
    projected = project(normed, w_qkv)
    ctx_index = lax.axis_index("ctx")
    positions = ctx_index * lat_rows + jnp.arange(lat_rows, dtype=jnp.int32)
    queries = rotate(projected[:, :query_width].reshape(lat_rows, HQ, HD), positions).astype(
        jnp.bfloat16
    )
    key_rows = rotate(
        projected[:, query_width : query_width + key_width].reshape(lat_rows, HK, HD), positions
    )
    key_rows = key_rows.astype(jnp.bfloat16).reshape(lat_rows, key_width)
    value_rows = projected[:, query_width + key_width :].astype(jnp.bfloat16)
    grouped = queries.reshape(lat_rows, HK, HQ // HK, HD)
    start_state = (
        jnp.full((HK, HQ // HK, lat_rows), masked_score, jnp.float32),
        jnp.zeros((HK, HQ // HK, lat_rows), jnp.float32),
        jnp.zeros((HK, HQ // HK, lat_rows, HD), jnp.float32),
    )
    key_all = lax.all_gather(key_rows, "ctx", axis=0, tiled=True)
    value_all = lax.all_gather(value_rows, "ctx", axis=0, tiled=True)
    blocks = key_all.shape[0] // lat_rows
    key_blocks = key_all.reshape(blocks, lat_rows, HK, HD)
    value_blocks = value_all.reshape(blocks, lat_rows, HK, HD)
    block_starts = lat_rows * jnp.arange(blocks, dtype=jnp.int32)

    def one_block(partial_value, block_data):
        key_block, value_block, key_start = block_data
        row_top, row_mass, weighted = partial_value
        scores = (
            jnp.einsum("qkgd,skd->kgqs", grouped, key_block, preferred_element_type=jnp.float32)
            * score_scale
        )
        key_pos = key_start + jnp.arange(lat_rows, dtype=jnp.int32)
        allowed = key_pos[None, :] <= positions[:, None]
        scores = jnp.where(allowed[None, None], scores, masked_score)
        new_top = jnp.maximum(row_top, jnp.max(scores, axis=-1))
        weights = jnp.exp(scores - new_top[..., None])
        shrink = jnp.exp(row_top - new_top)
        row_mass = row_mass * shrink + jnp.sum(weights, axis=-1)
        weighted = weighted * shrink[..., None] + jnp.einsum(
            "kgqs,skd->kgqd",
            weights.astype(jnp.bfloat16),
            value_block,
            preferred_element_type=jnp.float32,
        )
        return ((new_top, row_mass, weighted), None)

    result, unused = lax.scan(one_block, start_state, (key_blocks, value_blocks, block_starts))
    final_top, final_mass, final_sum = result
    attended = final_sum / final_mass[..., None]
    attended = jnp.transpose(attended, (2, 0, 1, 3)).reshape(lat_rows, HQ * HD).astype(jnp.bfloat16)
    branch = project(attended, w_out)
    hidden_out = (latent_wide + branch).astype(jnp.bfloat16)
    local_rows = align[0] - ctx_index * lat_rows
    picked = jnp.take(hidden_out, local_rows, axis=0)
    difference = picked.astype(jnp.float32) - teacher[0].astype(jnp.float32)
    token_loss = jnp.mean(difference * difference, axis=1)
    return (hidden_out[None], token_loss[None])


def rope_tables(blocks, rows):
    half = HD // 2
    frequency = np.float32(theta_base) ** (-np.arange(half, dtype=np.float32) * np.float32(2.0 / HD))
    places = [np.arange(rows), np.arange(blocks) * rows]
    angles = [np.concatenate([p[:, None] * frequency[None, :].astype(np.float64)] * 4, axis=1) for p in places]
    parts = [f(angles[0]) for f in (np.cos, np.sin)] + [f(angles[1]) for f in (np.cos, np.sin)]
    return np.concatenate(parts, axis=0).astype(np.float32)


def rope_at(rope_ref, rows, block):
    blocks = (rope_ref.shape[0] - 2 * rows) // 2
    cos, sin = rope_ref[:rows, :], rope_ref[rows : 2 * rows, :]
    cos_start = rope_ref[pl.ds(2 * rows + block, 1), :]
    sin_start = rope_ref[pl.ds(2 * rows + blocks + block, 1), :]
    lane = lax.broadcasted_iota(jnp.int32, (1, 128), 1)
    sign = jnp.where((lane & (HD // 2)) == 0, -1.0, 1.0)
    return (
        cos * cos_start - sin * sin_start,
        sin * (cos_start * sign) + cos * (sin_start * sign),
    )


def turn(x, cos, sin):
    half = HD // 2
    lane = lax.broadcasted_iota(jnp.int32, x.shape, 1)
    low = (lane & half) == 0
    swapped = jnp.where(low, pltpu.roll(x, 128 - half, axis=1), pltpu.roll(x, half, axis=1))
    return x * cos + swapped * sin


def part_kernel(where_ref, qkv_ref, align_ref, rope_ref, part_ref, align_out, rope_out):
    align_out[...] = align_ref[...]
    rope_out[...] = rope_ref[...]
    side = where_ref[2] % 2
    start = 0
    for width in (HQ * HD, HK * HD, HK * HD):
        own = width // 2
        part_ref[:, start // 2 : start // 2 + own] = qkv_ref[
            :, pl.ds(pl.multiple_of(start + side * own, own), own)
        ]
        start += width


def table_kernel(where_ref, bytes_ref, conv_ref, total_ref, out_ref):
    core = where_ref[1]
    taps_in = conv_ref.shape[0]
    half = total_ref.shape[0]
    rows = pl.ds(pl.multiple_of(core * half, half), half)
    mates = bytes_ref[rows, pl.ds(pl.multiple_of((1 - core) * taps_in, taps_in), taps_in)]
    total = total_ref[...] + jnp.dot(mates, conv_ref[...], preferred_element_type=jnp.float32)
    out_ref[...] = total.astype(jnp.bfloat16)


def one_hot_kernel(where_ref, ids_refs, hot_ref):
    side = where_ref[2] % 2
    length = ids_refs[0].shape[1]
    rows = length // KW
    row = lax.broadcasted_iota(jnp.int32, (rows, length), 0)
    mine = lax.broadcasted_iota(jnp.int32, (rows, length), 1) // KW == row
    tap = lax.broadcasted_iota(jnp.int32, (length, 128), 0) % KW
    pick = (tap == lax.broadcasted_iota(jnp.int32, (length, 128), 1)).astype(jnp.float32).astype(jnp.bfloat16)
    byte = lax.broadcasted_iota(jnp.int32, (rows, VOCAB), 1).astype(jnp.float32)
    for ids_ref, slot in zip(ids_refs, (2 + side, 3 - side, side, 1 - side)):
        ids = ids_ref[...].astype(jnp.float32)
        apart = jnp.where(mine, ids, 0.0).astype(jnp.bfloat16)
        columns = jnp.dot(apart, pick, preferred_element_type=jnp.float32)
        for k in range(KW):
            hot_ref[slot, :, k * VOCAB : (k + 1) * VOCAB] = (
                (columns[:, k : k + 1] == byte).astype(jnp.float32).astype(jnp.bfloat16)
            )


def ordered(chip, core, pieces):
    own, near, mate_own, mate_near = pieces
    depth = own.shape[0]
    for j, (mine, mates) in enumerate(zip((own,) + near, (mate_own,) + mate_near)):
        base = (chip ^ j) * 2
        for which, piece in ((core, mine), (1 - core, mates)):
            yield pl.ds(pl.multiple_of((base + which) * depth, depth), depth), piece


def attend(queries, slots, allowed, k_s, v_s, att_ref):
    heads = HQ // 2
    rows = att_ref.shape[0]
    keys = slice(slots[0] * rows, (slots[-1] + 1) * rows)

    def score(h):
        scores = lax.dot_general(
            k_s[h // GROUP, keys, :], queries(h), (((1,), (1,)), ((), ())), preferred_element_type=jnp.float32
        )
        last = jnp.where(allowed, scores[-rows:], masked_score)
        return last if len(slots) == 1 else jnp.concatenate([scores[:-rows], last], axis=0)

    coming, results = score(0), []
    for h in range(heads):
        scores = coming
        if h + 1 < heads:
            coming = score(h + 1)
        probs = jnp.exp(scores - jnp.max(scores, axis=0, keepdims=True)).astype(jnp.bfloat16)
        total = jnp.dot(v_s[h // GROUP, :, keys], probs, preferred_element_type=jnp.float32)
        results.append(total[:HD] / total[HD : HD + 1])
        if h % 2 == 1:
            pair = jnp.transpose(jnp.concatenate(results[-2:], axis=0))
            att_ref[:, (h - 1) * HD : (h + 1) * HD] = pair.astype(jnp.bfloat16)


def causal(rows):
    return lax.broadcasted_iota(jnp.int32, (rows, rows), 0) <= lax.broadcasted_iota(
        jnp.int32, (rows, rows), 1
    )


def key_variants(ctx, which):
    for block in range(2):
        now = tuple(range(2, 3 + block))
        yield (which == block) & (ctx < 2), block, now
        yield (which == block) & (ctx >= 2), block, (0, 1) + now


def latent_kernel(
    where_ref, hot_ref, own, near, mate_own, mate_near, gain_ref, normed_ref, lat_ref, table_s, lat_s,
):
    chip, core, ctx = where_ref[0], where_ref[1], where_ref[2]
    for span, piece in ordered(chip, core, (own, near, mate_own, mate_near)):
        table_s[span, :] = piece[...]
    gain = gain_ref[...].astype(jnp.float32)

    def latent_of(slot):
        latent = jnp.dot(hot_ref[slot], table_s[...], preferred_element_type=jnp.float32).astype(jnp.bfloat16)
        if slot >= 2:
            lat_s[slot - 2] = latent
        wide = latent.astype(jnp.float32)
        scale = lax.rsqrt(jnp.mean(wide * wide, axis=1, keepdims=True) + norm_eps)
        normed_ref[slot] = (wide * scale * gain).astype(jnp.bfloat16)

    @pl.when(ctx >= 2)
    def _():
        latent_of(0)
        latent_of(1)

    latent_of(2)
    latent_of(3)
    lat_ref[...] = lat_s[ctx % 2]


def lift_kernel(
    where_ref, normed_ref, own, near, mate_own, mate_near, rope_ref, att_ref, query_ref, k_s, v_s, weight_s, q_s,
):
    chip, core, ctx = where_ref[0], where_ref[1], where_ref[2]
    side, upper = ctx % 2, ctx // 2
    rows = att_ref.shape[0]
    q_width, k_width = HQ * HD // 2, HK * HD // 2
    for span, piece in ordered(chip, core, (own, near, mate_own, mate_near)):
        weight_s[span, :] = piece[...]
    v_s[:, HD:, :] = jnp.ones((v_s.shape[0], v_s.shape[1] - HD, v_s.shape[2]), jnp.bfloat16)

    def lift(slot):
        block = slot if slot < 2 else 2 * upper + slot - 2
        normed = normed_ref[slot]
        cos, sin = rope_at(rope_ref, rows, block)
        if slot >= 2:
            asked = jnp.dot(normed, weight_s[:, :q_width], preferred_element_type=jnp.float32)
            for pair in range(q_width // 128):
                turned = turn(asked[:, pair * 128 : (pair + 1) * 128], cos, sin)
                turned = (turned * score_scale).astype(jnp.bfloat16)
                q_s[slot - 2, 2 * pair] = turned[:, :HD]
                q_s[slot - 2, 2 * pair + 1] = turned[:, HD:]
        kept = jnp.dot(normed, weight_s[:, q_width:], preferred_element_type=jnp.float32)
        keys = turn(kept[:, :k_width], cos, sin).astype(jnp.bfloat16)
        values = jnp.transpose(kept[:, k_width:]).astype(jnp.bfloat16)
        for group in range(2):
            k_s[group, slot * rows : (slot + 1) * rows, :] = keys[:, group * HD : (group + 1) * HD]
            v_s[group, :HD, slot * rows : (slot + 1) * rows] = values[group * HD : (group + 1) * HD]

    @pl.when(upper == 1)
    def _():
        lift(0)
        lift(1)

    lift(2)
    lift(3)
    query_ref[...] = q_s[side]
    allowed = causal(rows)
    other = 1 - side
    for condition, block, slots in key_variants(ctx, other):

        @pl.when(condition)
        def _(block=block, slots=slots):
            attend(lambda h: q_s[block, h], slots, allowed, k_s, v_s, att_ref)


def own_kernel(where_ref, query_ref, k_ref, v_ref, att_ref):
    ctx = where_ref[2]
    allowed = causal(att_ref.shape[0])
    for condition, block, slots in key_variants(ctx, ctx % 2):

        @pl.when(condition)
        def _(slots=slots):
            attend(lambda h: query_ref[h], slots, allowed, k_ref, v_ref, att_ref)


def out_kernel(
    where_ref, own_att, mate_att, own, near, mate_own, mate_near, lat_ref, teacher_ref, align_ref,
    hidden_ref, loss_ref, att_s, weight_s,
):
    chip, core, ctx = where_ref[0], where_ref[1], where_ref[2]
    side = ctx % 2
    rows, width = lat_ref.shape
    part = own_att.shape[1]
    for span, piece in ordered(chip, core, (own, near, mate_own, mate_near)):
        weight_s[span, :] = piece[...]
    att_s[:, pl.ds(pl.multiple_of(side * part, part), part)] = own_att[...]
    att_s[:, pl.ds(pl.multiple_of((1 - side) * part, part), part)] = mate_att[...]
    branch = jnp.dot(att_s[...], weight_s[...], preferred_element_type=jnp.float32)
    hidden = (lat_ref[...].astype(jnp.float32) + branch).astype(jnp.bfloat16)
    hidden_ref[...] = hidden
    source = lax.broadcasted_iota(jnp.int32, (rows, rows), 0) + ctx * rows
    chosen = (source == align_ref[...]).astype(jnp.float32).astype(jnp.bfloat16)
    picked = lax.dot_general(
        chosen, hidden, (((0,), (0,)), ((), ())), preferred_element_type=jnp.float32
    )
    difference = picked - teacher_ref[...].astype(jnp.float32)
    square = difference * difference
    lanes = square[:, :128]
    for start in range(128, width, 128):
        lanes = lanes + square[:, start : start + 128]
    loss_ref[...] = jnp.sum(jnp.transpose(lanes), axis=0, keepdims=True) * (1.0 / width)


VMEM = pl.BlockSpec(memory_space=pltpu.VMEM)
SMEM = pl.BlockSpec(memory_space=pltpu.SMEM)
MIB = 1024 * 1024


def call(kernel, name, mib, flops, in_specs, outs, scratch=()):
    return pl.pallas_call(
        kernel,
        out_shape=tuple(jax.ShapeDtypeStruct(shape, dtype) for shape, dtype in outs),
        in_specs=in_specs,
        out_specs=(VMEM,) * len(outs),
        scratch_shapes=[pltpu.VMEM(shape, dtype) for shape, dtype in scratch],
        compiler_params=pltpu.CompilerParams(vmem_limit_bytes=mib * MIB),
        cost_estimate=pl.CostEstimate(flops=flops, bytes_accessed=4 * MIB, transcendentals=0),
        name=name,
    )


def head_body(sizes, byte_ids, byte_table, w_conv, w_qkv, w_out, norm_gain, teacher, align):
    n_fsdp, n_ctx = sizes
    me, ctx = lax.axis_index("fsdp"), lax.axis_index("ctx")
    chip, core = me // 2, me % 2
    rows = byte_ids.shape[1] // KW
    features = w_conv.shape[1]
    q_width = HQ * HD // 2
    part_width = w_qkv.shape[1] // 2
    half = VOCAB // 2
    bf16, f32 = jnp.bfloat16, jnp.float32
    where = jnp.stack([chip, core, ctx]).astype(jnp.int32)

    def swap(x, j):
        return lax.ppermute(x, "fsdp", [(d, d ^ j) for d in range(n_fsdp)])

    def along(x, pairs):
        return lax.ppermute(x, "ctx", pairs)

    def to_near(x):
        return tuple(swap(x, 2 * j) for j in range(1, n_fsdp // 2))

    def to_mate(x, near):
        return x, near, swap(x, 1), tuple(swap(piece, 1) for piece in near)

    beside = [(z, z ^ 1) for z in range(n_ctx)]

    mate_conv = swap(w_conv, 1)
    taps_in = w_conv.shape[0]
    mine = lax.dynamic_slice(byte_table, (core * half, core * taps_in), (half, taps_in))
    total = jnp.dot(mine, w_conv, preferred_element_type=f32)
    rope = jnp.asarray(rope_tables(n_ctx, rows))
    (own_t,) = call(
        table_kernel, "tap_table", 8, 10**8, [SMEM, VMEM, VMEM, VMEM], [((half, features), bf16)]
    )(where, byte_table, mate_conv, total)
    near_t = to_near(own_t)

    ids, late_qkv, unused = lax.optimization_barrier((byte_ids, w_qkv, own_t))
    ids_all = (
        ids,
        along(ids, beside),
        along(ids, [(0, 2), (1, 3)]),
        along(ids, [(0, 3), (1, 2)]),
    )
    part, align, rope = call(
        part_kernel, "qkv_part", 6, 10**8, [SMEM, VMEM, VMEM, VMEM],
        [((w_qkv.shape[0], part_width), bf16), (align.shape, jnp.int32), (rope.shape, f32)],
    )(where, late_qkv, align, rope)
    last, ids_all, part = lax.optimization_barrier((near_t[-1], ids_all, part))
    near_t = near_t[:-1] + (last,)
    part, unused = lax.optimization_barrier((part, near_t))
    near_w = to_near(part)

    (hot,) = call(
        one_hot_kernel, "one_hot", 8, 10**9, [SMEM, (VMEM,) * 4], [((n_ctx, rows, KW * VOCAB), bf16)]
    )(where, ids_all)
    near_specs = (VMEM,) * (n_fsdp // 2 - 1)
    piece_specs = [VMEM, near_specs, VMEM, near_specs]
    normed, latent = call(
        latent_kernel, "latents", 18, 2 * 10**9,
        [SMEM, VMEM] + piece_specs + [VMEM],
        [((n_ctx, rows, features), bf16), ((rows, features), bf16)],
        [((KW * VOCAB, features), bf16), ((2, rows, features), bf16)],
    )(where, hot, *to_mate(own_t, near_t), norm_gain[None])
    near_w, normed = lax.optimization_barrier((near_w, normed))
    out_own, unused = lax.optimization_barrier((w_out, near_w))
    out_near = to_near(out_own)

    att_shape = ((rows, q_width), bf16)
    att_mate, query, keys, values = call(
        lift_kernel, "lift", 16, 4 * 10**9,
        [SMEM, VMEM] + piece_specs + [VMEM],
        [
            att_shape,
            ((HQ // 2, rows, HD), bf16),
            ((2, 4 * rows, HD), bf16),
            ((2, HD + 16, 4 * rows), bf16),
        ],
        [((features, part_width), bf16), ((2, HQ // 2, rows, HD), bf16)],
    )(where, normed, *to_mate(part, near_w), rope)

    att_back = along(att_mate, beside)
    (att_own,) = call(
        own_kernel, "own_block", 12, 3 * 10**9, [SMEM, VMEM, VMEM, VMEM], [att_shape]
    )(where, query, keys, values)
    att_own, out_near = lax.optimization_barrier((att_own, out_near))
    hidden, loss = call(
        out_kernel, "project_out", 12, 10**9,
        [SMEM, VMEM, VMEM] + piece_specs + [VMEM, VMEM, VMEM],
        [((rows, features), bf16), ((1, rows), f32)],
        [((rows, features), bf16), ((features, features), bf16)],
    )(where, att_own, att_back, *to_mate(out_own, out_near), latent, teacher[0], align)
    return hidden[None], loss


def solution(mesh):
    in_specs = (
        P("fsdp", "ctx"),
        P(),
        P("fsdp", None),
        P("fsdp", None),
        P("fsdp", None),
        P(),
        P("fsdp", "ctx", None),
        P("fsdp", "ctx"),
    )
    out_specs = (P("fsdp", "ctx", None), P("fsdp", "ctx"))
    sizes = (mesh.shape["fsdp"], mesh.shape["ctx"])
    body = functools.partial(head_body, sizes) if sizes == (2 * KW, HK) else general_body
    return jax.shard_map(body, mesh=mesh, in_specs=in_specs, out_specs=out_specs, check_vma=False)
```

```python
import functools
import math

import jax
import jax.numpy as jnp
import numpy as np
from jax import lax
from jax.experimental import pallas as pl
from jax.experimental.pallas import tpu as pltpu
from jax.sharding import PartitionSpec as P

KW = 4
HQ = 16
HK = 4
HD = 64
GROUP = HQ // HK
VOCAB = 256

theta_base = 500000.0
norm_eps = 1e-05
masked_score = -1e30
score_scale = 1.0 / math.sqrt(HD)


def rotate(values, positions):
    half_dim = values.shape[-1] // 2
    frequency = theta_base ** (-jnp.arange(half_dim, dtype=jnp.float32) * 2.0 / values.shape[-1])
    angles = positions.astype(jnp.float32)[:, None] * frequency[None, :]
    angles = jnp.concatenate([angles, angles], axis=-1)[:, None, :]
    turned = jnp.concatenate([-values[..., half_dim:], values[..., :half_dim]], axis=-1)
    return values * jnp.cos(angles) + turned * jnp.sin(angles)


def project(inputs, weight):
    return jnp.dot(
        inputs,
        lax.all_gather(weight, "fsdp", axis=0, tiled=True),
        preferred_element_type=jnp.float32,
    )


def general_body(byte_ids, byte_table, w_conv, w_qkv, w_out, norm_gain, teacher, align):
    seq_bytes = byte_ids.shape[1]
    lat_rows = seq_bytes // KW
    query_width = HQ * HD
    key_width = HK * HD
    one_hot = (
        byte_ids[0][:, None] == jnp.arange(byte_table.shape[0], dtype=jnp.int32)[None, :]
    ).astype(jnp.bfloat16)
    embedded = jnp.dot(one_hot, byte_table, preferred_element_type=jnp.float32).astype(jnp.bfloat16)
    stacked = embedded.reshape(lat_rows, KW * byte_table.shape[1])
    latent = project(stacked, w_conv).astype(jnp.bfloat16)
    latent_wide = latent.astype(jnp.float32)
    scale_rows = lax.rsqrt(jnp.mean(latent_wide * latent_wide, axis=1, keepdims=True) + norm_eps)
    normed = (latent_wide * scale_rows * norm_gain.astype(jnp.float32)[None, :]).astype(
        jnp.bfloat16
    )
    projected = project(normed, w_qkv)
    ctx_index = lax.axis_index("ctx")
    positions = ctx_index * lat_rows + jnp.arange(lat_rows, dtype=jnp.int32)
    queries = rotate(projected[:, :query_width].reshape(lat_rows, HQ, HD), positions).astype(
        jnp.bfloat16
    )
    key_rows = rotate(
        projected[:, query_width : query_width + key_width].reshape(lat_rows, HK, HD), positions
    )
    key_rows = key_rows.astype(jnp.bfloat16).reshape(lat_rows, key_width)
    value_rows = projected[:, query_width + key_width :].astype(jnp.bfloat16)
    grouped = queries.reshape(lat_rows, HK, HQ // HK, HD)
    start_state = (
        jnp.full((HK, HQ // HK, lat_rows), masked_score, jnp.float32),
        jnp.zeros((HK, HQ // HK, lat_rows), jnp.float32),
        jnp.zeros((HK, HQ // HK, lat_rows, HD), jnp.float32),
    )
    key_all = lax.all_gather(key_rows, "ctx", axis=0, tiled=True)
    value_all = lax.all_gather(value_rows, "ctx", axis=0, tiled=True)
    blocks = key_all.shape[0] // lat_rows
    key_blocks = key_all.reshape(blocks, lat_rows, HK, HD)
    value_blocks = value_all.reshape(blocks, lat_rows, HK, HD)
    block_starts = lat_rows * jnp.arange(blocks, dtype=jnp.int32)

    def one_block(partial_value, block_data):
        key_block, value_block, key_start = block_data
        row_top, row_mass, weighted = partial_value
        scores = (
            jnp.einsum("qkgd,skd->kgqs", grouped, key_block, preferred_element_type=jnp.float32)
            * score_scale
        )
        key_pos = key_start + jnp.arange(lat_rows, dtype=jnp.int32)
        allowed = key_pos[None, :] <= positions[:, None]
        scores = jnp.where(allowed[None, None], scores, masked_score)
        new_top = jnp.maximum(row_top, jnp.max(scores, axis=-1))
        weights = jnp.exp(scores - new_top[..., None])
        shrink = jnp.exp(row_top - new_top)
        row_mass = row_mass * shrink + jnp.sum(weights, axis=-1)
        weighted = weighted * shrink[..., None] + jnp.einsum(
            "kgqs,skd->kgqd",
            weights.astype(jnp.bfloat16),
            value_block,
            preferred_element_type=jnp.float32,
        )
        return ((new_top, row_mass, weighted), None)

    result, unused = lax.scan(one_block, start_state, (key_blocks, value_blocks, block_starts))
    final_top, final_mass, final_sum = result
    attended = final_sum / final_mass[..., None]
    attended = jnp.transpose(attended, (2, 0, 1, 3)).reshape(lat_rows, HQ * HD).astype(jnp.bfloat16)
    branch = project(attended, w_out)
    hidden_out = (latent_wide + branch).astype(jnp.bfloat16)
    local_rows = align[0] - ctx_index * lat_rows
    picked = jnp.take(hidden_out, local_rows, axis=0)
    difference = picked.astype(jnp.float32) - teacher[0].astype(jnp.float32)
    token_loss = jnp.mean(difference * difference, axis=1)
    return (hidden_out[None], token_loss[None])


def rope_tables(blocks, rows):
    half = HD // 2
    frequency = np.float32(theta_base) ** (-np.arange(half, dtype=np.float32) * np.float32(2.0 / HD))
    places = [np.arange(rows), np.arange(blocks) * rows]
    angles = [np.concatenate([p[:, None] * frequency[None, :].astype(np.float64)] * 4, axis=1) for p in places]
    parts = [f(angles[0]) for f in (np.cos, np.sin)] + [f(angles[1]) for f in (np.cos, np.sin)]
    return np.concatenate(parts, axis=0).astype(np.float32)


def rope_at(rope_ref, rows, block):
    blocks = (rope_ref.shape[0] - 2 * rows) // 2
    cos, sin = rope_ref[:rows, :], rope_ref[rows : 2 * rows, :]
    cos_start = rope_ref[pl.ds(2 * rows + block, 1), :]
    sin_start = rope_ref[pl.ds(2 * rows + blocks + block, 1), :]
    lane = lax.broadcasted_iota(jnp.int32, (1, 128), 1)
    sign = jnp.where((lane & (HD // 2)) == 0, -1.0, 1.0)
    return (
        cos * cos_start - sin * sin_start,
        sin * (cos_start * sign) + cos * (sin_start * sign),
    )


def turn(x, cos, sin):
    half = HD // 2
    lane = lax.broadcasted_iota(jnp.int32, x.shape, 1)
    low = (lane & half) == 0
    swapped = jnp.where(low, pltpu.roll(x, 128 - half, axis=1), pltpu.roll(x, half, axis=1))
    return x * cos + swapped * sin


def part_kernel(where_ref, qkv_ref, align_ref, rope_ref, part_ref, align_out, rope_out):
    align_out[...] = align_ref[...]
    rope_out[...] = rope_ref[...]
    side = where_ref[2] % 2
    start = 0
    for width in (HQ * HD, HK * HD, HK * HD):
        own = width // 2
        part_ref[:, start // 2 : start // 2 + own] = qkv_ref[
            :, pl.ds(pl.multiple_of(start + side * own, own), own)
        ]
        start += width


def table_kernel(bytes_ref, conv_ref, total_ref, out_ref):
    total = total_ref[...] + jnp.dot(bytes_ref[...], conv_ref[...], preferred_element_type=jnp.float32)
    out_ref[...] = total.astype(jnp.bfloat16)


def one_hot_kernel(where_ref, ids_refs, hot_ref):
    side = where_ref[2] % 2
    length = ids_refs[0].shape[1]
    rows = length // KW
    row = lax.broadcasted_iota(jnp.int32, (rows, length), 0)
    mine = lax.broadcasted_iota(jnp.int32, (rows, length), 1) // KW == row
    tap = lax.broadcasted_iota(jnp.int32, (length, 128), 0) % KW
    pick = (tap == lax.broadcasted_iota(jnp.int32, (length, 128), 1)).astype(jnp.float32).astype(jnp.bfloat16)
    byte = lax.broadcasted_iota(jnp.int32, (rows, VOCAB), 1).astype(jnp.float32)
    for ids_ref, slot in zip(ids_refs, (2 + side, 3 - side, side, 1 - side)):
        ids = ids_ref[...].astype(jnp.float32)
        apart = jnp.where(mine, ids, 0.0).astype(jnp.bfloat16)
        columns = jnp.dot(apart, pick, preferred_element_type=jnp.float32)
        for k in range(KW):
            hot_ref[slot, :, k * VOCAB : (k + 1) * VOCAB] = (
                (columns[:, k : k + 1] == byte).astype(jnp.float32).astype(jnp.bfloat16)
            )


def ordered(chip, core, pieces):
    own, near, mate_own, mate_near = pieces
    depth = own.shape[0]
    for j, (mine, mates) in enumerate(zip((own,) + near, (mate_own,) + mate_near)):
        base = (chip ^ j) * 2
        for which, piece in ((core, mine), (1 - core, mates)):
            yield pl.ds(pl.multiple_of((base + which) * depth, depth), depth), piece


def attend(queries, slots, allowed, k_s, v_s, att_ref):
    heads = HQ // 2
    rows = att_ref.shape[0]
    keys = slice(slots[0] * rows, (slots[-1] + 1) * rows)

    def score(h):
        scores = lax.dot_general(
            k_s[h // GROUP, keys, :], queries(h), (((1,), (1,)), ((), ())), preferred_element_type=jnp.float32
        )
        last = jnp.where(allowed, scores[-rows:], masked_score)
        return last if len(slots) == 1 else jnp.concatenate([scores[:-rows], last], axis=0)

    coming, results = score(0), []
    for h in range(heads):
        scores = coming
        if h + 1 < heads:
            coming = score(h + 1)
        probs = jnp.exp(scores - jnp.max(scores, axis=0, keepdims=True)).astype(jnp.bfloat16)
        total = jnp.dot(v_s[h // GROUP, :, keys], probs, preferred_element_type=jnp.float32)
        results.append(total[:HD] / total[HD : HD + 1])
        if h % 2 == 1:
            pair = jnp.transpose(jnp.concatenate(results[-2:], axis=0))
            att_ref[:, (h - 1) * HD : (h + 1) * HD] = pair.astype(jnp.bfloat16)


def causal(rows):
    return lax.broadcasted_iota(jnp.int32, (rows, rows), 0) <= lax.broadcasted_iota(
        jnp.int32, (rows, rows), 1
    )


def key_variants(ctx, which):
    for block in range(2):
        now = tuple(range(2, 3 + block))
        yield (which == block) & (ctx < 2), block, now
        yield (which == block) & (ctx >= 2), block, (0, 1) + now


def latent_kernel(
    where_ref, hot_ref, own, near, mate_own, mate_near, gain_ref, normed_ref, lat_ref, table_s, lat_s,
):
    chip, core, ctx = where_ref[0], where_ref[1], where_ref[2]
    for span, piece in ordered(chip, core, (own, near, mate_own, mate_near)):
        table_s[span, :] = piece[...]
    gain = gain_ref[...].astype(jnp.float32)

    def latent_of(slot):
        latent = jnp.dot(hot_ref[slot], table_s[...], preferred_element_type=jnp.float32).astype(jnp.bfloat16)
        if slot >= 2:
            lat_s[slot - 2] = latent
        wide = latent.astype(jnp.float32)
        scale = lax.rsqrt(jnp.mean(wide * wide, axis=1, keepdims=True) + norm_eps)
        normed_ref[slot] = (wide * scale * gain).astype(jnp.bfloat16)

    @pl.when(ctx >= 2)
    def _():
        latent_of(0)
        latent_of(1)

    latent_of(2)
    latent_of(3)
    lat_ref[...] = lat_s[ctx % 2]


def lift_kernel(
    where_ref, normed_ref, own, near, mate_own, mate_near, rope_ref, att_ref, query_ref, k_s, v_s, weight_s, q_s,
):
    chip, core, ctx = where_ref[0], where_ref[1], where_ref[2]
    side, upper = ctx % 2, ctx // 2
    rows = att_ref.shape[0]
    q_width, k_width = HQ * HD // 2, HK * HD // 2
    for span, piece in ordered(chip, core, (own, near, mate_own, mate_near)):
        weight_s[span, :] = piece[...]
    v_s[:, HD:, :] = jnp.ones((v_s.shape[0], v_s.shape[1] - HD, v_s.shape[2]), jnp.bfloat16)

    def lift(slot):
        block = slot if slot < 2 else 2 * upper + slot - 2
        normed = normed_ref[slot]
        cos, sin = rope_at(rope_ref, rows, block)
        if slot >= 2:
            asked = jnp.dot(normed, weight_s[:, :q_width], preferred_element_type=jnp.float32)
            for pair in range(q_width // 128):
                turned = turn(asked[:, pair * 128 : (pair + 1) * 128], cos, sin)
                turned = (turned * score_scale).astype(jnp.bfloat16)
                q_s[slot - 2, 2 * pair] = turned[:, :HD]
                q_s[slot - 2, 2 * pair + 1] = turned[:, HD:]
        kept = jnp.dot(normed, weight_s[:, q_width:], preferred_element_type=jnp.float32)
        keys = turn(kept[:, :k_width], cos, sin).astype(jnp.bfloat16)
        values = jnp.transpose(kept[:, k_width:]).astype(jnp.bfloat16)
        for group in range(2):
            k_s[group, slot * rows : (slot + 1) * rows, :] = keys[:, group * HD : (group + 1) * HD]
            v_s[group, :HD, slot * rows : (slot + 1) * rows] = values[group * HD : (group + 1) * HD]

    @pl.when(upper == 1)
    def _():
        lift(0)
        lift(1)

    lift(2)
    lift(3)
    query_ref[...] = q_s[side]
    allowed = causal(rows)
    other = 1 - side
    for condition, block, slots in key_variants(ctx, other):

        @pl.when(condition)
        def _(block=block, slots=slots):
            attend(lambda h: q_s[block, h], slots, allowed, k_s, v_s, att_ref)


def own_kernel(where_ref, query_ref, k_ref, v_ref, att_ref):
    ctx = where_ref[2]
    allowed = causal(att_ref.shape[0])
    for condition, block, slots in key_variants(ctx, ctx % 2):

        @pl.when(condition)
        def _(slots=slots):
            attend(lambda h: query_ref[h], slots, allowed, k_ref, v_ref, att_ref)


def out_kernel(
    where_ref, own_att, mate_att, own, near, mate_own, mate_near, lat_ref, teacher_ref, align_ref,
    hidden_ref, loss_ref, att_s, weight_s,
):
    chip, core, ctx = where_ref[0], where_ref[1], where_ref[2]
    side = ctx % 2
    rows, width = lat_ref.shape
    part = own_att.shape[1]
    for span, piece in ordered(chip, core, (own, near, mate_own, mate_near)):
        weight_s[span, :] = piece[...]
    att_s[:, pl.ds(pl.multiple_of(side * part, part), part)] = own_att[...]
    att_s[:, pl.ds(pl.multiple_of((1 - side) * part, part), part)] = mate_att[...]
    branch = jnp.dot(att_s[...], weight_s[...], preferred_element_type=jnp.float32)
    hidden = (lat_ref[...].astype(jnp.float32) + branch).astype(jnp.bfloat16)
    hidden_ref[...] = hidden
    source = lax.broadcasted_iota(jnp.int32, (rows, rows), 0) + ctx * rows
    chosen = (source == align_ref[...]).astype(jnp.float32).astype(jnp.bfloat16)
    picked = lax.dot_general(
        chosen, hidden, (((0,), (0,)), ((), ())), preferred_element_type=jnp.float32
    )
    difference = picked - teacher_ref[...].astype(jnp.float32)
    square = difference * difference
    lanes = square[:, :128]
    for start in range(128, width, 128):
        lanes = lanes + square[:, start : start + 128]
    loss_ref[...] = jnp.sum(jnp.transpose(lanes), axis=0, keepdims=True) * (1.0 / width)


VMEM = pl.BlockSpec(memory_space=pltpu.VMEM)
SMEM = pl.BlockSpec(memory_space=pltpu.SMEM)
MIB = 1024 * 1024


def call(kernel, name, mib, flops, in_specs, outs, scratch=()):
    return pl.pallas_call(
        kernel,
        out_shape=tuple(jax.ShapeDtypeStruct(shape, dtype) for shape, dtype in outs),
        in_specs=in_specs,
        out_specs=(VMEM,) * len(outs),
        scratch_shapes=[pltpu.VMEM(shape, dtype) for shape, dtype in scratch],
        compiler_params=pltpu.CompilerParams(vmem_limit_bytes=mib * MIB),
        cost_estimate=pl.CostEstimate(flops=flops, bytes_accessed=4 * MIB, transcendentals=0),
        name=name,
    )


def head_body(sizes, byte_ids, byte_table, w_conv, w_qkv, w_out, norm_gain, teacher, align):
    n_fsdp, n_ctx = sizes
    me, ctx = lax.axis_index("fsdp"), lax.axis_index("ctx")
    chip, core = me // 2, me % 2
    rows = byte_ids.shape[1] // KW
    features = w_conv.shape[1]
    q_width = HQ * HD // 2
    part_width = w_qkv.shape[1] // 2
    half = VOCAB // 2
    bf16, f32 = jnp.bfloat16, jnp.float32
    where = jnp.stack([chip, core, ctx]).astype(jnp.int32)

    def swap(x, j):
        return lax.ppermute(x, "fsdp", [(d, d ^ j) for d in range(n_fsdp)])

    def along(x, pairs):
        return lax.ppermute(x, "ctx", pairs)

    def to_near(x):
        return tuple(swap(x, 2 * j) for j in range(1, n_fsdp // 2))

    def to_mate(x, near):
        return x, near, swap(x, 1), tuple(swap(piece, 1) for piece in near)

    beside = [(z, z ^ 1) for z in range(n_ctx)]

    mate_conv = swap(w_conv, 1)
    taps_in = w_conv.shape[0]
    mine = lax.dynamic_slice(byte_table, (core * half, core * taps_in), (half, taps_in))
    total = jnp.dot(mine, w_conv, preferred_element_type=f32)
    mates = lax.dynamic_slice(byte_table, (core * half, (1 - core) * taps_in), (half, taps_in))
    rope = jnp.asarray(rope_tables(n_ctx, rows))
    (own_t,) = call(
        table_kernel, "tap_table", 8, 10**8, [VMEM, VMEM, VMEM], [((half, features), bf16)]
    )(mates, mate_conv, total)
    near_t = to_near(own_t)

    ids, late_qkv, unused = lax.optimization_barrier((byte_ids, w_qkv, own_t))
    ids_all = (
        ids,
        along(ids, beside),
        along(ids, [(0, 2), (1, 3)]),
        along(ids, [(0, 3), (1, 2)]),
    )
    part, align, rope = call(
        part_kernel, "qkv_part", 6, 10**8, [SMEM, VMEM, VMEM, VMEM],
        [((w_qkv.shape[0], part_width), bf16), (align.shape, jnp.int32), (rope.shape, f32)],
    )(where, late_qkv, align, rope)
    last, ids_all, part = lax.optimization_barrier((near_t[-1], ids_all, part))
    near_t = near_t[:-1] + (last,)
    part, unused = lax.optimization_barrier((part, near_t))
    near_w = to_near(part)

    (hot,) = call(
        one_hot_kernel, "one_hot", 8, 10**9, [SMEM, (VMEM,) * 4], [((n_ctx, rows, KW * VOCAB), bf16)]
    )(where, ids_all)
    near_specs = (VMEM,) * (n_fsdp // 2 - 1)
    piece_specs = [VMEM, near_specs, VMEM, near_specs]
    normed, latent = call(
        latent_kernel, "latents", 18, 2 * 10**9,
        [SMEM, VMEM] + piece_specs + [VMEM],
        [((n_ctx, rows, features), bf16), ((rows, features), bf16)],
        [((KW * VOCAB, features), bf16), ((2, rows, features), bf16)],
    )(where, hot, *to_mate(own_t, near_t), norm_gain[None])
    near_w, normed = lax.optimization_barrier((near_w, normed))
    out_own, unused = lax.optimization_barrier((w_out, near_w))
    out_near = to_near(out_own)

    att_shape = ((rows, q_width), bf16)
    att_mate, query, keys, values = call(
        lift_kernel, "lift", 16, 4 * 10**9,
        [SMEM, VMEM] + piece_specs + [VMEM],
        [
            att_shape,
            ((HQ // 2, rows, HD), bf16),
            ((2, 4 * rows, HD), bf16),
            ((2, HD + 16, 4 * rows), bf16),
        ],
        [((features, part_width), bf16), ((2, HQ // 2, rows, HD), bf16)],
    )(where, normed, *to_mate(part, near_w), rope)

    att_back = along(att_mate, beside)
    (att_own,) = call(
        own_kernel, "own_block", 12, 3 * 10**9, [SMEM, VMEM, VMEM, VMEM], [att_shape]
    )(where, query, keys, values)
    att_own, out_near = lax.optimization_barrier((att_own, out_near))
    hidden, loss = call(
        out_kernel, "project_out", 12, 10**9,
        [SMEM, VMEM, VMEM] + piece_specs + [VMEM, VMEM, VMEM],
        [((rows, features), bf16), ((1, rows), f32)],
        [((rows, features), bf16), ((features, features), bf16)],
    )(where, att_own, att_back, *to_mate(out_own, out_near), latent, teacher[0], align)
    return hidden[None], loss


def solution(mesh):
    in_specs = (
        P("fsdp", "ctx"),
        P(),
        P("fsdp", None),
        P("fsdp", None),
        P("fsdp", None),
        P(),
        P("fsdp", "ctx", None),
        P("fsdp", "ctx"),
    )
    out_specs = (P("fsdp", "ctx", None), P("fsdp", "ctx"))
    sizes = (mesh.shape["fsdp"], mesh.shape["ctx"])
    body = functools.partial(head_body, sizes) if sizes == (2 * KW, HK) else general_body
    return jax.shard_map(body, mesh=mesh, in_specs=in_specs, out_specs=out_specs, check_vma=False)
```
